128 devices in a mesh: seq: 128 (over z, x, y, core).
Axes of the slice: x: 4, y: 4, z: 4, core: 2. Of those that a mesh axis runs over, the one named last changes fastest.
Arguments:
- hidden: bfloat16 [65536, 2560], P('seq'), may hold values from -6 to 6
- w_bc: bfloat16 [2560, 256], replicated, may hold values from -0.009765625 to 0.009765625
- ssm_in: bfloat16 [65536, 2560], P('seq'), may hold values from -6 to 6
- codes: int32 [40, 65536], P(None, 'seq'), may hold values from 0 to 2000, as said below
- rates: float32 [40], replicated, as said below
- skip: float32 [40], replicated, may hold values from 0.5 to 1.5
- grad_out: bfloat16 [65536, 2560], P('seq'), may hold values from -6 to 6
Outputs:
- mixed: bfloat16 [65536, 2560], P('seq')
- grad_x: bfloat16 [65536, 2560], P('seq')
- grad_w: float32 [2560, 256], replicated
The draws below stay inside these ranges and needn't reach their ends.
Inputs may be any that keep to these rules, and one draw needn't show every extreme that they name: Decay codes; codes above 1000 mark sudden losses of state. Positive decay rates.
All inputs are finite; a program needn't handle non-finite values.
Results may differ from the reference program's by a relative error of at most 0.011.
Values sent between devices are 32-bit elements; how exact they have to be, the bound alone decides.
No kernel may reach another device: no remote copies, remote signals or barrier semaphores. Data moves between devices by JAX's collectives and lax.ppermute only.
A program may use at most 704 MiB of HBM per device.

```python
import jax
import jax.numpy as jnp
from jax import lax

D = 2560
H = 40
P_SIZE = 64
N = 128
TOK_DEV = 512
DOCUMENT_TOKENS = 65536
N_SEQ = 128


def draw_codes(key, part):
    first_key = jax.random.fold_in(key, 11)
    secondary_random_key = jax.random.fold_in(key, 23)
    baseline_symbols = jax.random.randint(first_key, (H, DOCUMENT_TOKENS), 0, 1001)
    spike_locations = jax.random.randint(secondary_random_key, (6,), 0, DOCUMENT_TOKENS)
    token_offsets = jnp.arange(DOCUMENT_TOKENS)
    spike_flags = jnp.any(token_offsets[None, :] == spike_locations[:, None], axis=0)
    return jnp.where(spike_flags[None, :], 2000, baseline_symbols).astype(jnp.int32)


def draw_rates(key, part):
    first_key = jax.random.fold_in(key, 31)
    low_log = jnp.log(jnp.float32(0.01) / DOCUMENT_TOKENS)
    return jnp.exp(jax.random.uniform(first_key, (H,), jnp.float32, low_log, jnp.log(jnp.float32(0.05))))


def level_of(rng, shape, shards, smallest, top_value):
    factor_of, own = 1.0, jax.random.fold_in(rng, 6)
    for axis_at, parts in shards:
        heights = jnp.exp(jax.random.uniform(jax.random.fold_in(own, axis_at), (parts,), jnp.float32, smallest / len(shards), top_value / len(shards)))
        factor_of = factor_of * jnp.repeat(heights, shape[axis_at] // parts).reshape([-1 if axis == axis_at else 1 for axis in range(len(shape))])
    return factor_of


def normal_values(stream_key, shape, scale, reach, cuts=(), kind=jnp.bfloat16):
    array = scale * jax.random.normal(stream_key, shape, jnp.float32)
    if cuts:
        array = array * level_of(stream_key, shape, cuts, -0.22, 0.18)
    return jnp.clip(array, -reach, reach).astype(kind)


def setup_inputs(seed: int = 0) -> dict:
    splits = jax.random.split(jax.random.key(seed), 8)
    return {
        "hidden": normal_values(splits[0], (DOCUMENT_TOKENS, D), 1.0, 6.0, ((0, 128),)),
        "w_bc": normal_values(splits[1], (D, 2 * N), (D * N) ** -0.5, 0.009765625),
        "ssm_in": normal_values(splits[2], (DOCUMENT_TOKENS, H * P_SIZE), 1.0, 6.0, ((0, 128),)),
        "codes": draw_codes(jax.random.fold_in(splits[7], 71), 0),
        "rates": draw_rates(jax.random.fold_in(splits[7], 71), 0),
        "skip": jnp.clip(1.0 + 0.1 * jax.random.normal(splits[5], (H,), jnp.float32), 0.5, 1.5),
        "grad_out": normal_values(splits[6], (DOCUMENT_TOKENS, H * P_SIZE), 1.0, 6.0, ((0, 128),)),
    }


def log_decay(code_block, rates):
    code_value = code_block.astype(jnp.float32)
    return -(rates[:, None] * jnp.minimum(code_value, 1000.0) / 1000.0 + 0.0005 * jnp.maximum(code_value - 1000.0, 0.0))


def block_maps(hidden_blk, w_bc, code_blk, rates):
    bc_proj = jnp.dot(hidden_blk, w_bc, preferred_element_type=jnp.float32).astype(jnp.bfloat16)
    b_mat = bc_proj[:, :N]
    c_mat = bc_proj[:, N:]
    cumulative = jnp.cumsum(log_decay(code_blk, rates), axis=1)
    total_log = cumulative[:, -1]
    return b_mat, c_mat, cumulative, total_log


def weighted_terms(x_blk, dy_blk, cumulative, total_log):
    weighted_in = (x_blk.astype(jnp.float32) * jnp.exp(total_log[:, None] - cumulative).T[:, :, None]).astype(jnp.bfloat16)
    weighted_grad = (dy_blk.astype(jnp.float32) * jnp.exp(cumulative).T[:, :, None]).astype(jnp.bfloat16)
    return weighted_in, weighted_grad


def reference(hidden, w_bc, ssm_in, codes, rates, skip, grad_out):
    block_count = N_SEQ
    tok_count = TOK_DEV
    hidden_b = hidden.reshape(block_count, tok_count, D)
    x_b = ssm_in.reshape(block_count, tok_count, H, P_SIZE)
    dy_b = grad_out.reshape(block_count, tok_count, H, P_SIZE)
    code_b = codes.reshape(H, block_count, tok_count).transpose(1, 0, 2)
    highest = lax.Precision.HIGHEST

    def local_terms(block_in):
        hidden_blk, x_blk, dy_blk, code_blk = block_in
        b_mat, c_mat, cumulative, total_log = block_maps(hidden_blk, w_bc, code_blk, rates)
        weighted_in, weighted_grad = weighted_terms(x_blk, dy_blk, cumulative, total_log)
        s_fwd = jnp.einsum('lhp,ln->hpn', weighted_in.astype(jnp.float32), b_mat.astype(jnp.float32))
        s_back = jnp.einsum('lhp,ln->hpn', weighted_grad.astype(jnp.float32), c_mat.astype(jnp.float32))
        return jnp.exp(total_log), s_fwd, s_back

    decay_all, forward_state_gathered, sback_all = lax.map(local_terms, (hidden_b, x_b, dy_b, code_b))

    def advance(state, pieces):
        decay_total, contrib = pieces
        return decay_total[:, None, None] * state + contrib, state

    zero_state = jnp.zeros((H, P_SIZE, N), jnp.float32)
    _, s_prev_all = lax.scan(advance, zero_state, (decay_all, forward_state_gathered))
    _, g_next_all = lax.scan(advance, zero_state, (decay_all, sback_all), reverse=True)

    lower_mask = jnp.arange(tok_count)[:, None] >= jnp.arange(tok_count)[None, :]

    def finish(grad_sum, block_in):
        hidden_blk, x_blk, dy_blk, code_blk, s_prev, g_next = block_in
        b_mat, c_mat, cumulative, total_log = block_maps(hidden_blk, w_bc, code_blk, rates)
        weighted_in, weighted_grad = weighted_terms(x_blk, dy_blk, cumulative, total_log)
        x_float = x_blk.astype(jnp.float32)
        dy_float = dy_blk.astype(jnp.float32)
        scores = jnp.dot(c_mat, b_mat.T, preferred_element_type=jnp.float32)
        log_gap = cumulative[:, :, None] - cumulative[:, None, :]
        decay = jnp.exp(jnp.where(lower_mask[None], log_gap, -jnp.inf))
        mixing = (scores[None] * decay).astype(jnp.bfloat16)
        y_intra = jnp.einsum('hts,shp->thp', mixing.astype(jnp.float32), x_float)
        dx_intra = jnp.einsum('hts,thp->shp', mixing.astype(jnp.float32), dy_float)
        pair_dots = jnp.einsum('thp,shp->hts', dy_float, x_float)
        kmat = jnp.sum(decay * pair_dots, axis=0).astype(jnp.bfloat16)
        dc_intra = jnp.dot(kmat, b_mat, preferred_element_type=jnp.float32)
        db_intra = jnp.dot(kmat.T, c_mat, preferred_element_type=jnp.float32)
        y_carry = jnp.exp(cumulative).T[:, :, None] * jnp.einsum('tn,hpn->thp', c_mat.astype(jnp.float32), s_prev, precision=highest)
        dx_carry = jnp.exp(total_log[:, None] - cumulative).T[:, :, None] * jnp.einsum('tn,hpn->thp', b_mat.astype(jnp.float32), g_next, precision=highest)
        dc_carry = jnp.einsum('thp,hpn->tn', weighted_grad.astype(jnp.float32), s_prev, precision=highest)
        db_carry = jnp.einsum('thp,hpn->tn', weighted_in.astype(jnp.float32), g_next, precision=highest)
        mixed = (y_intra + y_carry + skip[None, :, None] * x_float).astype(jnp.bfloat16).reshape(tok_count, H * P_SIZE)
        grad_x = (dx_intra + dx_carry + skip[None, :, None] * dy_float).astype(jnp.bfloat16).reshape(tok_count, H * P_SIZE)
        dbc = jnp.concatenate([db_intra + db_carry, dc_intra + dc_carry], axis=1).astype(jnp.bfloat16)
        weight_part = jnp.einsum('ld,lk->dk', hidden_blk.astype(jnp.float32), dbc.astype(jnp.float32))
        return grad_sum + weight_part, (mixed, grad_x)

    grad_sum, (mixed_all, gradx_all) = lax.scan(finish, jnp.zeros((D, 2 * N), jnp.float32), (hidden_b, x_b, dy_b, code_b, s_prev_all, g_next_all))
    grad_w = grad_sum / DOCUMENT_TOKENS
    return mixed_all.reshape(DOCUMENT_TOKENS, H * P_SIZE), gradx_all.reshape(DOCUMENT_TOKENS, H * P_SIZE), grad_w
```

```python
import functools

import jax
import jax.numpy as jnp
from jax import lax
from jax.experimental import pallas as pl
from jax.experimental.pallas import tpu as pltpu
from jax.sharding import Mesh
from jax.sharding import PartitionSpec as P

F32 = jnp.float32
BF16 = jnp.bfloat16
CHIP_AXES = ("z", "x", "y")
ALL_AXES = ("z", "x", "y", "c")
T = 512
H = 40
PS = 64
N = 128
D = 2560
G = 4
GH = H // G
GL = GH * PS
GT = GL // 128
NM = N // 8
CHIPS = 64
STATE_ROWS = 8 * GT
ROWS = 48
HALF_D = D // 2
GW_ROWS = 40


def mm(a, b):
    return jnp.dot(a, b, preferred_element_type=F32)


def mm_nt(a, b):
    return lax.dot_general(a, b, (((1,), (1,)), ((), ())), preferred_element_type=F32)


def mm_tn(a, b):
    return lax.dot_general(a, b, (((0,), (0,)), ((), ())), preferred_element_type=F32)


def spread_matrix():
    k = lax.broadcasted_iota(jnp.int32, (128, GL), 0)
    col = lax.broadcasted_iota(jnp.int32, (128, GL), 1)
    return jnp.where((k & 63) == (col >> 6), 1.0, 0.0).astype(BF16)


def spread(v, onehot):
    high = v.astype(BF16).astype(F32)
    low = pltpu.roll(v - high, 64, 1)
    lane = lax.broadcasted_iota(jnp.int32, v.shape, 1)
    return mm(jnp.where(lane < 64, high, low).astype(BF16), onehot)


def pre_kernel(
    c_ref, hidden_ref, w_ref, x_ref, dy_ref, codes_ref, rates_ref,
    bc_ref, cum_ref, cumt_ref, state_ref, cum_scr, group_scr,
):
    q = pl.program_id(0)
    core = c_ref[0]

    @pl.when(q == 0)
    def _():
        bc_ref[...] = mm(hidden_ref[...], w_ref[...]).astype(BF16)
        code = codes_ref[...].astype(F32)
        step = -(
            rates_ref[...] * jnp.minimum(code, 1000.0) / 1000.0
            + 0.0005 * jnp.maximum(code - 1000.0, 0.0)
        )
        s_at = lax.broadcasted_iota(jnp.int32, (T, T), 0)
        t_at = lax.broadcasted_iota(jnp.int32, (T, T), 1)
        upper = jnp.where(s_at <= t_at, 1.0, 0.0).astype(BF16)
        p1 = step.astype(BF16)
        rest = step - p1.astype(F32)
        p2 = rest.astype(BF16)
        p3 = (rest - p2.astype(F32)).astype(BF16)
        cum_scr[...] = mm(p1, upper) + mm(p2, upper) + mm(p3, upper)
        group_scr[...] = jnp.zeros_like(group_scr)

    for i in range(G):

        @pl.when(q == i)
        def _(i=i):
            group_scr[0:GH, :] = cum_scr[GH * i : GH * (i + 1), :]

    cum_ref[0] = group_scr[0:16, :]
    cumt = group_scr[...].T
    cumt_ref[0] = cumt
    onehot = spread_matrix()
    total = cumt[T - 1 : T, :]
    fwd_weight = jnp.exp(cumt)
    back_weight = jnp.exp(total - cumt)
    b_mat = bc_ref[:, :N]
    c_mat = bc_ref[:, N:]
    fw = spread(fwd_weight, onehot)
    bw = spread(back_weight, onehot)
    wi = (x_ref[...].astype(F32) * bw).astype(BF16)
    wg = (dy_ref[...].astype(F32) * fw).astype(BF16)
    sf = mm_tn(b_mat, wi)
    sb = mm_tn(c_mat, wg)
    decay = fw[T - 8 : T, :]
    for chain, state in ((0, sf), (1, sb)):
        slot = jnp.bitwise_xor(chain, core)
        for m in range(NM):
            for i in range(GT):
                state_ref[slot, m, 8 * i : 8 * i + 8, :] = state[
                    8 * m : 8 * m + 8, 128 * i : 128 * i + 128
                ]
            for i in range(GT):
                state_ref[slot, m, STATE_ROWS + i : STATE_ROWS + i + 1, :] = decay[
                    7:8, 128 * i : 128 * i + 128
                ]
            state_ref[slot, m, STATE_ROWS + GT : ROWS, :] = jnp.zeros(
                (ROWS - STATE_ROWS - GT, 128), F32
            )


def pre(core, hidden, w_bc, x, dy, codes, rates):
    full = lambda *shape: pl.BlockSpec(shape, lambda q: (0,) * len(shape))
    cols = pl.BlockSpec((T, GL), lambda q: (0, q))
    return pl.pallas_call(
        pre_kernel,
        grid=(G,),
        in_specs=[
            pl.BlockSpec(memory_space=pltpu.SMEM),
            full(T, D),
            full(D, 2 * N),
            cols,
            cols,
            full(H, T),
            full(H, 1),
        ],
        out_specs=[
            full(T, 2 * N),
            pl.BlockSpec((1, 16, T), lambda q: (q, 0, 0)),
            pl.BlockSpec((1, T, 128), lambda q: (q, 0, 0)),
            pl.BlockSpec((2, NM, ROWS, 128), lambda q: (0, q, 0, 0)),
        ],
        out_shape=[
            jax.ShapeDtypeStruct((T, 2 * N), BF16),
            jax.ShapeDtypeStruct((G, 16, T), F32),
            jax.ShapeDtypeStruct((G, T, 128), F32),
            jax.ShapeDtypeStruct((2, CHIPS, ROWS, 128), F32),
        ],
        scratch_shapes=[pltpu.VMEM((H, T), F32), pltpu.VMEM((128, T), F32)],
        compiler_params=pltpu.CompilerParams(vmem_limit_bytes=40 << 20),
        cost_estimate=pl.CostEstimate(
            flops=2 * 10**9, bytes_accessed=13 * 10**6, transcendentals=0
        ),
        name="pre",
    )(core, hidden, w_bc, x, dy, codes, rates)


def chip_kernel(mine_ref, got_ref, out_ref):
    for m in range(NM):
        for i in range(GT):
            other = got_ref[m, STATE_ROWS + i : STATE_ROWS + i + 1, :]
            rows = slice(8 * i, 8 * i + 8)
            out_ref[m, rows, :] = other * mine_ref[m, rows, :] + got_ref[m, rows, :]
        tail = slice(STATE_ROWS, ROWS)
        out_ref[m, tail, :] = mine_ref[m, tail, :] * got_ref[m, tail, :]


def chip_sum(mine, got):
    spec = pl.BlockSpec((NM, ROWS, 128), lambda q: (q, 0, 0))
    return pl.pallas_call(
        chip_kernel,
        grid=(G,),
        in_specs=[spec, spec],
        out_specs=spec,
        out_shape=jax.ShapeDtypeStruct((CHIPS, ROWS, 128), F32),
        name="chip_sum",
    )(mine, got)


def scan_kernel(c_ref, in_ref, out_ref):
    core = c_ref[0]
    state = [jnp.zeros((8, 128), F32) for _ in range(GT)]
    for k in range(CHIPS):
        at = k + core * (CHIPS - 1 - 2 * k)
        for i in range(GT):
            rows = slice(8 * i, 8 * i + 8)
            out_ref[at, rows, :] = state[i]
            decay = in_ref[at, STATE_ROWS + i : STATE_ROWS + i + 1, :]
            state[i] = decay * state[i] + in_ref[at, rows, :]


def scan_chips(core, slices):
    return pl.pallas_call(
        scan_kernel,
        in_specs=[
            pl.BlockSpec(memory_space=pltpu.SMEM),
            pl.BlockSpec(memory_space=pltpu.VMEM),
        ],
        out_specs=pl.BlockSpec(memory_space=pltpu.VMEM),
        out_shape=jax.ShapeDtypeStruct((CHIPS, STATE_ROWS, 128), F32),
        name="scan_chips",
    )(core, slices)


def pass_kernel(mine_ref, came_ref, out_ref):
    for m in range(NM):
        for i in range(GT):
            own = mine_ref[m, STATE_ROWS + i : STATE_ROWS + i + 1, :]
            rows = slice(8 * i, 8 * i + 8)
            out_ref[m, rows, :] = own * came_ref[m, rows, :] + mine_ref[m, rows, :]


def pass_on(mine, came):
    spec = lambda rows: pl.BlockSpec((NM, rows, 128), lambda q: (q, 0, 0))
    return pl.pallas_call(
        pass_kernel,
        grid=(G,),
        in_specs=[spec(ROWS), spec(STATE_ROWS)],
        out_specs=spec(STATE_ROWS),
        out_shape=jax.ShapeDtypeStruct((CHIPS, STATE_ROWS, 128), F32),
        name="pass_on",
    )(mine, came)


def intra_kernel(
    bc_ref, x_ref, dy_ref, cum_ref, cumt_ref, skip_ref,
    ybase_ref, dxbase_ref, wi_ref, wg_ref, dbc_ref, scores, kmat, yacc, dxacc,
):
    q = pl.program_id(0)
    b_mat = bc_ref[:, :N]
    c_mat = bc_ref[:, N:]

    @pl.when(q == 0)
    def _():
        scores[...] = mm_nt(c_mat, b_mat)
        kmat[...] = jnp.zeros_like(kmat)

    onehot = spread_matrix()
    cumt = cumt_ref[0]
    x = x_ref[...].astype(F32)
    dy = dy_ref[...].astype(F32)
    skip = skip_ref[...]
    fw = spread(jnp.exp(cumt), onehot)
    wg_ref[...] = (dy * fw).astype(BF16)
    bw = spread(jnp.exp(cumt[T - 1 : T, :] - cumt), onehot)
    wi_ref[...] = (x * bw).astype(BF16)
    yacc[...] = skip * x
    dxacc[...] = skip * dy
    for start, size in ((0, 256), (0, 128), (256, 128)):
        lo = slice(start, start + size)
        hi = slice(start + size, start + 2 * size)
        edge = cumt[start + size - 1 : start + size, :]
        u_lo = spread(jnp.exp(edge - cumt[lo, :]), onehot)
        u_hi = spread(jnp.exp(cumt[hi, :] - edge), onehot)
        xs = (x[lo, :] * u_lo).astype(BF16)
        dys = (dy[hi, :] * u_hi).astype(BF16)
        pair = scores[hi, lo].astype(BF16)
        kmat[hi, lo] += mm_nt(dys, xs)
        yacc[hi, :] += u_hi * mm(pair, xs)
        dxacc[lo, :] += u_lo * mm_tn(pair, dys)
    size = 128
    t_at = lax.broadcasted_iota(jnp.int32, (size, size), 0)
    s_at = lax.broadcasted_iota(jnp.int32, (size, size), 1)
    lower = t_at >= s_at
    first = s_at < PS
    for chunk in range(T // size):
        rows = slice(chunk * size, (chunk + 1) * size)
        score = scores[rows, rows]
        ksum = jnp.zeros((size, size), F32)
        for i in range(GT):
            lanes = slice(128 * i, 128 * i + 128)
            xt = x_ref[rows, lanes]
            dyt = dy_ref[rows, lanes]
            dyf = dy[rows, lanes]
            ys, dxs = [], []
            for e in range(2):
                h = 2 * i + e
                gap = cumt[rows, h : h + 1] - cum_ref[0, h : h + 1, rows]
                decay = jnp.exp(jnp.where(lower, gap, -jnp.inf))
                mixing = (score * decay).astype(BF16)
                own = first if e == 0 else jnp.logical_not(first)
                dyh = jnp.where(own, dyf, 0.0).astype(BF16)
                ksum += decay * mm_nt(dyh, xt)
                ys.append(mm(mixing, xt))
                dxs.append(mm_tn(mixing, dyt))
            yacc[rows, lanes] += jnp.where(first, ys[0], ys[1])
            dxacc[rows, lanes] += jnp.where(first, dxs[0], dxs[1])
        kmat[rows, rows] += ksum
    ybase_ref[...] = yacc[...].astype(ybase_ref.dtype)
    dxbase_ref[...] = dxacc[...].astype(dxbase_ref.dtype)

    @pl.when(q == G - 1)
    def _():
        k = kmat[...].astype(BF16)
        dbc_ref[:, :N] = mm_tn(k, c_mat)
        dbc_ref[:, N:] = mm(k, b_mat)


def intra(bc, x, dy, cum, cumt, skip_row):
    full = lambda *shape: pl.BlockSpec(shape, lambda q: (0,) * len(shape))
    cols = pl.BlockSpec((T, GL), lambda q: (0, q))
    return pl.pallas_call(
        intra_kernel,
        grid=(G,),
        in_specs=[
            full(T, 2 * N),
            cols,
            cols,
            pl.BlockSpec((1, 16, T), lambda q: (q, 0, 0)),
            pl.BlockSpec((1, T, 128), lambda q: (q, 0, 0)),
            pl.BlockSpec((1, GL), lambda q: (0, q)),
        ],
        out_specs=[cols, cols, cols, cols, full(T, 2 * N)],
        out_shape=[
            jax.ShapeDtypeStruct((T, D), F32),
            jax.ShapeDtypeStruct((T, D), F32),
            jax.ShapeDtypeStruct((T, D), BF16),
            jax.ShapeDtypeStruct((T, D), BF16),
            jax.ShapeDtypeStruct((T, 2 * N), F32),
        ],
        scratch_shapes=[
            pltpu.VMEM((T, T), F32),
            pltpu.VMEM((T, T), F32),
            pltpu.VMEM((T, GL), F32),
            pltpu.VMEM((T, GL), F32),
        ],
        compiler_params=pltpu.CompilerParams(vmem_limit_bytes=48 << 20),
        cost_estimate=pl.CostEstimate(
            flops=25 * 10**9, bytes_accessed=26 * 10**6, transcendentals=3 * 10**6
        ),
        name="intra",
    )(bc, x, dy, cum, cumt, skip_row)


def finish_kernel(
    c_ref, bc_ref, came_ref, got_ref, ybase_ref, dxbase_ref, wi_ref, wg_ref, cumt_ref,
    dbc_ref, hidden_ref, mixed_ref, gradx_ref, gw_ref, sfs, sbs, acc,
):
    q = pl.program_id(0)
    core = c_ref[0]
    is_first = core == 0

    @pl.when(q == 0)
    def _():
        acc[...] = dbc_ref[...]

    for m in range(NM // 2):
        for i in range(GT):
            rows = slice(8 * i, 8 * i + 8)
            lanes = slice(128 * i, 128 * i + 128)
            came = jnp.concatenate([came_ref[2 * m, rows, :], came_ref[2 * m + 1, rows, :]])
            got = jnp.concatenate([got_ref[2 * m, rows, :], got_ref[2 * m + 1, rows, :]])
            at = slice(16 * m, 16 * m + 16)
            sfs[at, lanes] = jnp.where(is_first, came, got).astype(BF16)
            sbs[at, lanes] = jnp.where(is_first, got, came).astype(BF16)
    b_mat = bc_ref[:, :N]
    c_mat = bc_ref[:, N:]
    onehot = spread_matrix()
    cumt = cumt_ref[0]
    s_prev = sfs[...]
    g_next = sbs[...]
    fw = spread(jnp.exp(cumt), onehot)
    mixed_ref[...] = (ybase_ref[...].astype(F32) + fw * mm(c_mat, s_prev)).astype(BF16)
    bw = spread(jnp.exp(cumt[T - 1 : T, :] - cumt), onehot)
    gradx_ref[...] = (dxbase_ref[...].astype(F32) + bw * mm(b_mat, g_next)).astype(BF16)
    acc[:, :N] += mm_nt(wi_ref[...], g_next)
    acc[:, N:] += mm_nt(wg_ref[...], s_prev)

    @pl.when(q == G - 1)
    def _():
        dbc = acc[...].astype(BF16)
        for half in range(2):
            slot = jnp.bitwise_xor(half, core)
            part = mm_tn(hidden_ref[:, HALF_D * half : HALF_D * (half + 1)], dbc)
            part = part * (1.0 / (T * 2 * CHIPS))
            gw_ref[slot, 0] = part[:, :N]
            gw_ref[slot, 1] = part[:, N:]


def finish(core, bc, came, got, ybase, dxbase, wi, wg, cumt, dbc, hidden):
    full = lambda *shape: pl.BlockSpec(shape, lambda q: (0,) * len(shape))
    cols = pl.BlockSpec((T, GL), lambda q: (0, q))
    state = pl.BlockSpec((NM, STATE_ROWS, 128), lambda q: (q, 0, 0))
    return pl.pallas_call(
        finish_kernel,
        grid=(G,),
        in_specs=[
            pl.BlockSpec(memory_space=pltpu.SMEM),
            full(T, 2 * N),
            state,
            state,
            cols,
            cols,
            cols,
            cols,
            pl.BlockSpec((1, T, 128), lambda q: (q, 0, 0)),
            full(T, 2 * N),
            full(T, D),
        ],
        out_specs=[cols, cols, full(2, 2, HALF_D, N)],
        out_shape=[
            jax.ShapeDtypeStruct((T, D), BF16),
            jax.ShapeDtypeStruct((T, D), BF16),
            jax.ShapeDtypeStruct((2, 2, HALF_D, N), F32),
        ],
        scratch_shapes=[
            pltpu.VMEM((N, GL), BF16),
            pltpu.VMEM((N, GL), BF16),
            pltpu.VMEM((T, 2 * N), F32),
        ],
        compiler_params=pltpu.CompilerParams(vmem_limit_bytes=48 << 20),
        cost_estimate=pl.CostEstimate(
            flops=3 * 10**9, bytes_accessed=26 * 10**6, transcendentals=0
        ),
        name="finish",
    )(core, bc, came, got, ybase, dxbase, wi, wg, cumt, dbc, hidden)


def add_kernel(a_ref, b_ref, out_ref):
    out_ref[...] = a_ref[...] + b_ref[...]


def pair_add(a, b):
    spec = pl.BlockSpec((16, GW_ROWS, 128), lambda q: (q, 0, 0))
    return pl.pallas_call(
        add_kernel,
        grid=(4,),
        in_specs=[spec, spec],
        out_specs=spec,
        out_shape=jax.ShapeDtypeStruct((CHIPS, GW_ROWS, 128), F32),
        name="pair_add",
    )(a, b)


def total_kernel(in_ref, out_ref):
    total = jnp.sum(in_ref[...], axis=0)
    for k in range(CHIPS):
        out_ref[k] = total


def chip_total(parts):
    return pl.pallas_call(
        total_kernel,
        in_specs=[pl.BlockSpec(memory_space=pltpu.VMEM)],
        out_specs=pl.BlockSpec(memory_space=pltpu.VMEM),
        out_shape=jax.ShapeDtypeStruct((CHIPS, GW_ROWS, 128), F32),
        name="chip_total",
    )(parts)


def place_kernel(c_ref, mine_ref, got_ref, out_ref):
    half = pl.program_id(0)
    is_mine = half == c_ref[0]
    for lane in range(2):
        out_ref[:, 128 * lane : 128 * lane + 128] = jnp.where(
            is_mine, mine_ref[lane], got_ref[lane]
        )


def place(core, mine, got):
    block = 256
    spec = pl.BlockSpec((2, block, 128), lambda half, i: (0, i, 0))
    return pl.pallas_call(
        place_kernel,
        grid=(2, HALF_D // block),
        in_specs=[pl.BlockSpec(memory_space=pltpu.SMEM), spec, spec],
        out_specs=pl.BlockSpec(
            (block, 2 * N), lambda half, i: (half * (HALF_D // block) + i, 0)
        ),
        out_shape=jax.ShapeDtypeStruct((D, 2 * N), F32),
        name="place",
    )(core, mine, got)


def swap(v):
    return lax.ppermute(v, "c", [(0, 1), (1, 0)])


def exchange(v):
    return lax.all_to_all(v, CHIP_AXES, 0, 0, tiled=True)


def shards(hidden, w_bc, ssm_in, codes, rates, skip, grad_out):
    core = lax.axis_index("c").astype(jnp.int32).reshape(1)
    skip_row = jnp.repeat(skip, PS)[None, :]
    bc, cum, cumt, states = pre(
        core, hidden, w_bc, ssm_in, grad_out, codes, rates.reshape(H, 1)
    )
    mine = states[0]
    got = swap(states[1])
    slices = exchange(chip_sum(mine, got))
    ybase, dxbase, wi, wg, dbc = intra(bc, ssm_in, grad_out, cum, cumt, skip_row)
    came = exchange(scan_chips(core, slices))
    other = swap(pass_on(mine, came))
    mixed, gradx, gw = finish(
        core, bc, came, other, ybase, dxbase, wi, wg, cumt, dbc, hidden
    )
    gw = gw.reshape(2, CHIPS, GW_ROWS, 128)
    part = pair_add(gw[0], swap(gw[1]))
    half = exchange(chip_total(exchange(part))).reshape(2, HALF_D, 128)
    grad_w = place(core, half, swap(half))
    return mixed, gradx, grad_w


def solution(mesh):
    grid = Mesh(mesh.devices.reshape(4, 4, 4, 2), ALL_AXES)
    rows = P(ALL_AXES, None)
    return jax.shard_map(
        shards,
        mesh=grid,
        in_specs=(rows, P(), rows, P(None, ALL_AXES), P(), P(), rows),
        out_specs=(rows, rows, P()),
        check_vma=False,
    )
```

```python
import functools

import jax
import jax.numpy as jnp
from jax import lax
from jax.experimental import pallas as pl
from jax.experimental.pallas import tpu as pltpu
from jax.sharding import Mesh
from jax.sharding import PartitionSpec as P

F32 = jnp.float32
BF16 = jnp.bfloat16
CHIP_AXES = ("z", "x", "y")
ALL_AXES = ("z", "x", "y", "c")
T = 512
H = 40
PS = 64
N = 128
D = 2560
G = 4
GH = H // G
GL = GH * PS
GT = GL // 128
NM = N // 8
CHIPS = 64
STATE_ROWS = 8 * GT
ROWS = 48
HALF_D = D // 2
GW_ROWS = 40
LARGE = 56 << 20
SMALL = 10 << 20
WHOLE = pl.BlockSpec(memory_space=pltpu.VMEM)


def mm(a, b):
    return jnp.dot(a, b, preferred_element_type=F32)


def mm_nt(a, b):
    return lax.dot_general(a, b, (((1,), (1,)), ((), ())), preferred_element_type=F32)


def mm_tn(a, b):
    return lax.dot_general(a, b, (((0,), (0,)), ((), ())), preferred_element_type=F32)


def spread_matrix():
    k = lax.broadcasted_iota(jnp.int32, (128, GL), 0)
    col = lax.broadcasted_iota(jnp.int32, (128, GL), 1)
    return jnp.where((k & 63) == (col >> 6), 1.0, 0.0).astype(BF16)


def spread(v, onehot):
    high = v.astype(BF16).astype(F32)
    low = pltpu.roll(v - high, 64, 1)
    lane = lax.broadcasted_iota(jnp.int32, v.shape, 1)
    return mm(jnp.where(lane < 64, high, low).astype(BF16), onehot)


def token_spec():
    return pl.BlockSpec((8, 128), lambda *_: (0, 0))


def token_shape():
    return jax.ShapeDtypeStruct((8, 128), F32)


def pre_kernel(
    c_ref, hidden_hbm, w_hbm, x_hbm, dy_hbm, codes_ref, rates_ref,
    bc_ref, cum_ref, cumt_ref, mine_hbm, other_hbm,
    hidden_scr, w_scr, x_scr, dy_scr, mine_scr, other_scr, group_scr, in_sem, out_sem,
):
    is_first = c_ref[0] == 0
    cols = [pl.ds(GL * q, GL) for q in range(G)]
    slices = [pl.ds(NM * q, NM) for q in range(G)]
    loads = []
    for q in range(G):
        for n, (src, dst) in enumerate(
            (
                (hidden_hbm.at[:, cols[q]], hidden_scr.at[q]),
                (w_hbm.at[cols[q], :], w_scr.at[q]),
                (x_hbm.at[:, cols[q]], x_scr.at[q]),
                (dy_hbm.at[:, cols[q]], dy_scr.at[q]),
            )
        ):
            loads.append(pltpu.make_async_copy(src, dst, in_sem.at[n, q]))
    for pick in ((0, 1), (2, 3)):
        for q in range(G):
            for n in pick:
                loads[4 * q + n].start()

    eye = lax.broadcasted_iota(jnp.int32, (H, H), 0) == lax.broadcasted_iota(
        jnp.int32, (H, H), 1
    )
    rates = jnp.sum(jnp.where(eye, rates_ref[...], 0.0), axis=1, keepdims=True)
    code = codes_ref[...].astype(F32)
    step = -(
        rates * jnp.minimum(code, 1000.0) / 1000.0
        + 0.0005 * jnp.maximum(code - 1000.0, 0.0)
    )
    s_at = lax.broadcasted_iota(jnp.int32, (T, T), 0)
    t_at = lax.broadcasted_iota(jnp.int32, (T, T), 1)
    upper = jnp.where(s_at <= t_at, 1.0, 0.0).astype(BF16)
    p1 = step.astype(BF16)
    rest = step - p1.astype(F32)
    p2 = rest.astype(BF16)
    p3 = (rest - p2.astype(F32)).astype(BF16)
    cum = mm(p1, upper) + mm(p2, upper) + mm(p3, upper)
    group_scr[...] = jnp.zeros_like(group_scr)
    onehot = spread_matrix()
    for q in range(G):
        group_scr[q, 0:GH, :] = cum[GH * q : GH * (q + 1), :]
        cum_ref[q] = group_scr[q, 0:16, :]
        cumt_ref[q] = group_scr[q].T

    acc = None
    for q in range(G):
        loads[4 * q].wait()
        loads[4 * q + 1].wait()
        part = mm(hidden_scr[q], w_scr[q])
        acc = part if acc is None else acc + part
    bc_ref[...] = acc.astype(BF16)

    stores = []
    for q in range(G):
        cumt = cumt_ref[q]
        fw = spread(jnp.exp(cumt), onehot)
        bw = spread(jnp.exp(cumt[T - 1 : T, :] - cumt), onehot)
        loads[4 * q + 2].wait()
        wi = (x_scr[q].astype(F32) * bw).astype(BF16)
        loads[4 * q + 3].wait()
        wg = (dy_scr[q].astype(F32) * fw).astype(BF16)
        sf = mm_tn(bc_ref[:, :N], wi)
        sb = mm_tn(bc_ref[:, N:], wg)
        decay = fw[T - 1 : T, :]
        for n, (scr, hbm, state) in enumerate(
            (
                (other_scr, other_hbm, jnp.where(is_first, sb, sf)),
                (mine_scr, mine_hbm, jnp.where(is_first, sf, sb)),
            )
        ):
            for m in range(NM):
                for i in range(GT):
                    lanes = slice(128 * i, 128 * i + 128)
                    scr[NM * q + m, 8 * i : 8 * i + 8, :] = state[8 * m : 8 * m + 8, lanes]
                    row = STATE_ROWS + i
                    scr[NM * q + m, row : row + 1, :] = decay[:, lanes]
                scr[NM * q + m, STATE_ROWS + GT : ROWS, :] = jnp.zeros(
                    (ROWS - STATE_ROWS - GT, 128), F32
                )
            stores.append(
                pltpu.make_async_copy(
                    scr.at[slices[q]], hbm.at[slices[q]], out_sem.at[n, q]
                )
            )
            stores[-1].start()
    for store in stores:
        store.wait()


def pre(core, hidden, w_bc, x, dy, codes, rates):
    hbm = pl.BlockSpec(memory_space=pl.ANY)
    return pl.pallas_call(
        pre_kernel,
        in_specs=[pl.BlockSpec(memory_space=pltpu.SMEM)] + [hbm] * 4 + [WHOLE] * 2,
        out_specs=[WHOLE] * 3 + [hbm] * 2,
        out_shape=[
            jax.ShapeDtypeStruct((T, 2 * N), BF16),
            jax.ShapeDtypeStruct((G, 16, T), F32),
            jax.ShapeDtypeStruct((G, T, 128), F32),
            jax.ShapeDtypeStruct((CHIPS, ROWS, 128), F32),
            jax.ShapeDtypeStruct((CHIPS, ROWS, 128), F32),
        ],
        scratch_shapes=[
            pltpu.VMEM((G, T, GL), BF16),
            pltpu.VMEM((G, GL, 2 * N), BF16),
            pltpu.VMEM((G, T, GL), BF16),
            pltpu.VMEM((G, T, GL), BF16),
            pltpu.VMEM((CHIPS, ROWS, 128), F32),
            pltpu.VMEM((CHIPS, ROWS, 128), F32),
            pltpu.VMEM((G, 128, T), F32),
            pltpu.SemaphoreType.DMA((4, G)),
            pltpu.SemaphoreType.DMA((2, G)),
        ],
        compiler_params=pltpu.CompilerParams(vmem_limit_bytes=LARGE),
        cost_estimate=pl.CostEstimate(
            flops=2 * 10**9, bytes_accessed=13 * 10**6, transcendentals=0
        ),
        name="pre",
    )(core, hidden, w_bc, x, dy, codes, rates)


def chip_kernel(mine_ref, got_ref, out_ref, token_ref):
    for m in range(CHIPS):
        for i in range(GT):
            other = got_ref[m, STATE_ROWS + i : STATE_ROWS + i + 1, :]
            rows = slice(8 * i, 8 * i + 8)
            out_ref[m, rows, :] = other * mine_ref[m, rows, :] + got_ref[m, rows, :]
        tail = slice(STATE_ROWS, ROWS)
        out_ref[m, tail, :] = mine_ref[m, tail, :] * got_ref[m, tail, :]
    token_ref[...] = jnp.zeros_like(token_ref)


def chip_sum(mine, got):
    return pl.pallas_call(
        chip_kernel,
        in_specs=[WHOLE, WHOLE],
        out_specs=[WHOLE, WHOLE],
        out_shape=[jax.ShapeDtypeStruct((CHIPS, ROWS, 128), F32), token_shape()],
        compiler_params=pltpu.CompilerParams(vmem_limit_bytes=SMALL),
        name="chip_sum",
    )(mine, got)


def scan_kernel(c_ref, in_ref, token_ref, out_ref):
    core = c_ref[0]
    state = [jnp.zeros((8, 128), F32) for _ in range(GT)]
    for k in range(CHIPS):
        at = k + core * (CHIPS - 1 - 2 * k)
        for i in range(GT):
            rows = slice(8 * i, 8 * i + 8)
            out_ref[at, rows, :] = state[i]
            decay = in_ref[at, STATE_ROWS + i : STATE_ROWS + i + 1, :]
            state[i] = decay * state[i] + in_ref[at, rows, :]


def scan_chips(core, slices, token):
    return pl.pallas_call(
        scan_kernel,
        in_specs=[pl.BlockSpec(memory_space=pltpu.SMEM), WHOLE, WHOLE],
        out_specs=WHOLE,
        out_shape=jax.ShapeDtypeStruct((CHIPS, STATE_ROWS, 128), F32),
        compiler_params=pltpu.CompilerParams(vmem_limit_bytes=SMALL),
        name="scan_chips",
    )(core, slices, token)


SPANS = ((0, 256), (0, 128), (256, 128))
CHUNK = 128


def span_weights(cumt, onehot, start, size):
    lo = slice(start, start + size)
    hi = slice(start + size, start + 2 * size)
    edge = cumt[start + size - 1 : start + size, :]
    u_lo = spread(jnp.exp(edge - cumt[lo, :]), onehot)
    u_hi = spread(jnp.exp(cumt[hi, :] - edge), onehot)
    return lo, hi, u_lo, u_hi


def chunk_masks():
    t_at = lax.broadcasted_iota(jnp.int32, (CHUNK, CHUNK), 0)
    s_at = lax.broadcasted_iota(jnp.int32, (CHUNK, CHUNK), 1)
    return t_at >= s_at, s_at < PS


def chunk_decay(cumt, cum_ref, rows, h, lower):
    gap = cumt[rows, h : h + 1] - cum_ref[0, h : h + 1, rows]
    return jnp.exp(jnp.where(lower, gap, -jnp.inf))


def pairs_kernel(
    c_ref, bc_ref, x_ref, dy_ref, cum_ref, cumt_ref, hidden_ref, after_ref,
    wmine_ref, wother_ref, dbc_ref, turned_ref, token_ref, kmat,
):
    q = pl.program_id(0)
    is_first = c_ref[0] == 0

    @pl.when(q == 0)
    def _():
        kmat[...] = jnp.zeros_like(kmat)

    turned_ref[...] = hidden_ref[...].T
    onehot = spread_matrix()
    cumt = cumt_ref[0]
    x = x_ref[...].astype(F32)
    dy = dy_ref[...].astype(F32)
    wg = dy * spread(jnp.exp(cumt), onehot)
    wi = x * spread(jnp.exp(cumt[T - 1 : T, :] - cumt), onehot)
    wmine_ref[...] = jnp.where(is_first, wg, wi).astype(BF16)
    wother_ref[...] = jnp.where(is_first, wi, wg).astype(BF16)
    for start, size in SPANS:
        lo, hi, u_lo, u_hi = span_weights(cumt, onehot, start, size)
        kmat[hi, lo] += mm_nt((dy[hi, :] * u_hi).astype(BF16), (x[lo, :] * u_lo).astype(BF16))
    lower, first = chunk_masks()
    for chunk in range(T // CHUNK):
        rows = slice(chunk * CHUNK, (chunk + 1) * CHUNK)
        ksum = jnp.zeros((CHUNK, CHUNK), F32)
        for i in range(GT):
            lanes = slice(128 * i, 128 * i + 128)
            xt = x_ref[rows, lanes]
            dyf = dy[rows, lanes]
            for e in range(2):
                own = first if e == 0 else jnp.logical_not(first)
                dyh = jnp.where(own, dyf, 0.0).astype(BF16)
                ksum += chunk_decay(cumt, cum_ref, rows, 2 * i + e, lower) * mm_nt(dyh, xt)
        kmat[rows, rows] += ksum

    @pl.when(q == G - 1)
    def _():
        k = kmat[...].astype(BF16)
        dbc_ref[:, :N] = mm_tn(k, bc_ref[:, N:])
        dbc_ref[:, N:] = mm(k, bc_ref[:, :N])
        token_ref[...] = jnp.zeros_like(token_ref)


def full_spec(*shape):
    return pl.BlockSpec(shape, lambda q: (0,) * len(shape))


def cols_spec(rows=T):
    return pl.BlockSpec((rows, GL), lambda q: (0, q))


def group_spec(*shape):
    return pl.BlockSpec((1, *shape), lambda q: (q, 0, 0))


def pairs(core, bc, x, dy, cum, cumt, hidden, token):
    return pl.pallas_call(
        pairs_kernel,
        grid=(G,),
        in_specs=[
            pl.BlockSpec(memory_space=pltpu.SMEM),
            full_spec(T, 2 * N),
            cols_spec(),
            cols_spec(),
            group_spec(16, T),
            group_spec(T, 128),
            cols_spec(),
            token_spec(),
        ],
        out_specs=[
            cols_spec(),
            cols_spec(),
            full_spec(T, 2 * N),
            pl.BlockSpec((GL, T), lambda q: (q, 0)),
            token_spec(),
        ],
        out_shape=[
            jax.ShapeDtypeStruct((T, D), BF16),
            jax.ShapeDtypeStruct((T, D), BF16),
            jax.ShapeDtypeStruct((T, 2 * N), F32),
            jax.ShapeDtypeStruct((D, T), BF16),
            token_shape(),
        ],
        scratch_shapes=[pltpu.VMEM((T, T), F32)],
        compiler_params=pltpu.CompilerParams(vmem_limit_bytes=LARGE),
        cost_estimate=pl.CostEstimate(
            flops=20 * 10**9, bytes_accessed=16 * 10**6, transcendentals=3 * 10**6
        ),
        name="pairs",
    )(core, bc, x, dy, cum, cumt, hidden, token)


def carry_kernel(w_ref, came_ref, acc_ref, state_ref):
    acc = jnp.zeros((T, N), F32)
    for q in range(G):
        for i in range(GT):
            rows = slice(8 * i, 8 * i + 8)
            lanes = slice(GL * q + 128 * i, GL * q + 128 * i + 128)
            for m in range(0, NM, 2):
                at = NM * q + m
                pair = jnp.concatenate([came_ref[at, rows, :], came_ref[at + 1, rows, :]])
                state_ref[8 * m : 8 * m + 16, lanes] = pair.astype(BF16)
        cols = slice(GL * q, GL * (q + 1))
        acc += mm_nt(w_ref[:, cols], state_ref[:, cols])
    acc_ref[...] = acc


def carry(w_mine, came):
    return pl.pallas_call(
        carry_kernel,
        in_specs=[WHOLE, WHOLE],
        out_specs=[WHOLE, WHOLE],
        out_shape=[
            jax.ShapeDtypeStruct((T, N), F32),
            jax.ShapeDtypeStruct((N, D), BF16),
        ],
        compiler_params=pltpu.CompilerParams(vmem_limit_bytes=SMALL),
        cost_estimate=pl.CostEstimate(
            flops=4 * 10**8, bytes_accessed=5 * 10**6, transcendentals=0
        ),
        name="carry",
    )(w_mine, came)


def weight_kernel(
    c_ref, accmine_ref, wother_ref, came_ref, theirs_ref, dbc_ref, turned_ref,
    gwmine_ref, gwother_ref, state_ref,
):
    core = c_ref[0]
    is_first = core == 0
    acc = jnp.zeros((T, N), F32)
    for q in range(G):
        for i in range(GT):
            rows = slice(8 * i, 8 * i + 8)
            lanes = slice(GL * q + 128 * i, GL * q + 128 * i + 128)
            tail = slice(STATE_ROWS + i, STATE_ROWS + i + 1)
            decay = theirs_ref[NM * q, tail, :]
            for m in range(0, NM, 2):
                at = NM * q + m
                pair = jnp.concatenate(
                    [
                        decay * came_ref[a, rows, :] + theirs_ref[a, rows, :]
                        for a in (at, at + 1)
                    ]
                )
                state_ref[8 * m : 8 * m + 16, lanes] = pair.astype(BF16)
        cols = slice(GL * q, GL * (q + 1))
        acc += mm_nt(wother_ref[:, cols], state_ref[:, cols])
    mine = accmine_ref[...]
    db = dbc_ref[:, :N] + jnp.where(is_first, acc, mine)
    dc = dbc_ref[:, N:] + jnp.where(is_first, mine, acc)
    dbc = (jnp.concatenate([db, dc], axis=1) * (1.0 / (T * 2 * CHIPS))).astype(BF16)
    for ref, half in ((gwother_ref, 1 - core), (gwmine_ref, core)):
        start = pl.multiple_of(half * HALF_D, HALF_D)
        part = mm(turned_ref[pl.ds(start, HALF_D), :], dbc)
        ref[0] = part[:, :N]
        ref[1] = part[:, N:]


def weight_part(core, acc_mine, w_other, came, theirs, dbc, turned):
    return pl.pallas_call(
        weight_kernel,
        in_specs=[pl.BlockSpec(memory_space=pltpu.SMEM)] + [WHOLE] * 6,
        out_specs=[WHOLE, WHOLE, WHOLE],
        out_shape=[
            jax.ShapeDtypeStruct((2, HALF_D, N), F32),
            jax.ShapeDtypeStruct((2, HALF_D, N), F32),
            jax.ShapeDtypeStruct((N, D), BF16),
        ],
        compiler_params=pltpu.CompilerParams(vmem_limit_bytes=20 << 20),
        cost_estimate=pl.CostEstimate(
            flops=2 * 10**9, bytes_accessed=12 * 10**6, transcendentals=0
        ),
        name="weight_part",
    )(core, acc_mine, w_other, came, theirs, dbc, turned)


def outputs_kernel(
    c_ref, bc_ref, x_ref, dy_ref, cum_ref, cumt_ref, skip_ref, smine_ref, sother_ref, after_ref,
    mixed_ref, gradx_ref, token_ref, scores, yacc, dxacc,
):
    is_first = c_ref[0] == 0
    b_mat = bc_ref[:, :N]
    c_mat = bc_ref[:, N:]

    @pl.when(pl.program_id(0) == 0)
    def _():
        scores[...] = mm_nt(c_mat, b_mat)

    onehot = spread_matrix()
    cumt = cumt_ref[0]
    x = x_ref[...].astype(F32)
    dy = dy_ref[...].astype(F32)
    skip = skip_ref[...]
    mine = smine_ref[...].astype(F32)
    other = sother_ref[...].astype(F32)
    s_prev = jnp.where(is_first, mine, other).astype(BF16)
    g_next = jnp.where(is_first, other, mine).astype(BF16)
    fw = spread(jnp.exp(cumt), onehot)
    yacc[...] = skip * x + fw * mm(c_mat, s_prev)
    bw = spread(jnp.exp(cumt[T - 1 : T, :] - cumt), onehot)
    dxacc[...] = skip * dy + bw * mm(b_mat, g_next)
    for start, size in SPANS:
        lo, hi, u_lo, u_hi = span_weights(cumt, onehot, start, size)
        pair = scores[hi, lo].astype(BF16)
        yacc[hi, :] += u_hi * mm(pair, (x[lo, :] * u_lo).astype(BF16))
        dxacc[lo, :] += u_lo * mm_tn(pair, (dy[hi, :] * u_hi).astype(BF16))
    lower, first = chunk_masks()
    for chunk in range(T // CHUNK):
        rows = slice(chunk * CHUNK, (chunk + 1) * CHUNK)
        score = scores[rows, rows]
        for i in range(GT):
            lanes = slice(128 * i, 128 * i + 128)
            xt = x_ref[rows, lanes]
            dyt = dy_ref[rows, lanes]
            ys, dxs = [], []
            for e in range(2):
                decay = chunk_decay(cumt, cum_ref, rows, 2 * i + e, lower)
                mixing = (score * decay).astype(BF16)
                ys.append(mm(mixing, xt))
                dxs.append(mm_tn(mixing, dyt))
            mixed_ref[rows, lanes] = (
                yacc[rows, lanes] + jnp.where(first, ys[0], ys[1])
            ).astype(BF16)
            gradx_ref[rows, lanes] = (
                dxacc[rows, lanes] + jnp.where(first, dxs[0], dxs[1])
            ).astype(BF16)
    token_ref[...] = jnp.zeros_like(token_ref)


def outputs(core, bc, x, dy, cum, cumt, skip_row, s_mine, s_other, token):
    return pl.pallas_call(
        outputs_kernel,
        grid=(G,),
        in_specs=[
            pl.BlockSpec(memory_space=pltpu.SMEM),
            full_spec(T, 2 * N),
            cols_spec(),
            cols_spec(),
            group_spec(16, T),
            group_spec(T, 128),
            cols_spec(1),
            cols_spec(N),
            cols_spec(N),
            token_spec(),
        ],
        out_specs=[cols_spec(), cols_spec(), token_spec()],
        out_shape=[
            jax.ShapeDtypeStruct((T, D), BF16),
            jax.ShapeDtypeStruct((T, D), BF16),
            token_shape(),
        ],
        scratch_shapes=[
            pltpu.VMEM((T, T), F32),
            pltpu.VMEM((T, GL), F32),
            pltpu.VMEM((T, GL), F32),
        ],
        compiler_params=pltpu.CompilerParams(vmem_limit_bytes=LARGE),
        cost_estimate=pl.CostEstimate(
            flops=25 * 10**9, bytes_accessed=13 * 10**6, transcendentals=3 * 10**6
        ),
        name="outputs",
    )(core, bc, x, dy, cum, cumt, skip_row, s_mine, s_other, token)


def add_kernel(a_ref, b_ref, out_ref, token_ref):
    out_ref[...] = a_ref[...] + b_ref[...]
    token_ref[...] = jnp.zeros_like(token_ref)


def pair_add(a, b):
    return pl.pallas_call(
        add_kernel,
        in_specs=[WHOLE, WHOLE],
        out_specs=[WHOLE, WHOLE],
        out_shape=[jax.ShapeDtypeStruct(a.shape, F32), token_shape()],
        compiler_params=pltpu.CompilerParams(vmem_limit_bytes=SMALL),
        name="pair_add",
    )(a, b)


def total_kernel(in_ref, token_ref, out_ref):
    total = jnp.sum(in_ref[...], axis=0)
    for k in range(CHIPS):
        out_ref[k] = total


def chip_total(parts, token):
    return pl.pallas_call(
        total_kernel,
        in_specs=[WHOLE, WHOLE],
        out_specs=WHOLE,
        out_shape=jax.ShapeDtypeStruct((CHIPS, GW_ROWS, 128), F32),
        compiler_params=pltpu.CompilerParams(vmem_limit_bytes=SMALL),
        name="chip_total",
    )(parts, token)


def place_kernel(c_ref, half_ref, *refs):
    out_ref = refs[-1]
    for lane in range(2):
        out_ref[:, 128 * lane : 128 * lane + 128] = half_ref[lane]


def place(at, half, into):
    block = HALF_D // 2
    extra = [] if into is None else [into]
    return pl.pallas_call(
        place_kernel,
        grid_spec=pltpu.PrefetchScalarGridSpec(
            num_scalar_prefetch=1,
            grid=(2,),
            in_specs=[pl.BlockSpec((2, block, 128), lambda i, c: (0, i, 0))]
            + [pl.BlockSpec(memory_space=pl.ANY)] * len(extra),
            out_specs=pl.BlockSpec((block, 2 * N), lambda i, c: (2 * c[0] + i, 0)),
        ),
        out_shape=jax.ShapeDtypeStruct((D, 2 * N), F32),
        input_output_aliases={2: 0} if extra else {},
        compiler_params=pltpu.CompilerParams(vmem_limit_bytes=SMALL),
        name="place",
    )(at, half, *extra)


def swap(v):
    return lax.ppermute(v, "c", [(0, 1), (1, 0)])


def exchange(v):
    return lax.all_to_all(v, CHIP_AXES, 0, 0, tiled=True)


def shards(hidden, w_bc, ssm_in, codes, rates, skip, grad_out):
    core = lax.axis_index("c").astype(jnp.int32).reshape(1)
    skip_row = jnp.repeat(skip, PS)[None, :]
    bc, cum, cumt, mine, other = pre(
        core, hidden, w_bc, ssm_in, grad_out, codes, rates[None, :]
    )
    chip, token = chip_sum(mine, swap(other))
    slices = exchange(chip)
    theirs = swap(mine)
    w_mine, w_other, dbc, turned, token = pairs(
        core, bc, ssm_in, grad_out, cum, cumt, hidden, token
    )
    came = exchange(scan_chips(core, slices, token))
    acc_mine, s_mine = carry(w_mine, came)
    gw_mine, gw_other, s_other = weight_part(
        core, acc_mine, w_other, swap(came), theirs, dbc, turned
    )
    part, token = pair_add(gw_mine, swap(gw_other))
    sums = exchange(part.reshape(CHIPS, GW_ROWS, 128))
    mixed, gradx, token = outputs(
        core, bc, ssm_in, grad_out, cum, cumt, skip_row, s_mine, s_other, token
    )
    half = exchange(chip_total(sums, token)).reshape(2, HALF_D, 128)
    grad_w = place(1 - core, swap(half), place(core, half, None))
    return mixed, gradx, grad_w


def solution(mesh):
    grid = Mesh(mesh.devices.reshape(4, 4, 4, 2), ALL_AXES)
    rows = P(ALL_AXES, None)
    return jax.shard_map(
        shards,
        mesh=grid,
        in_specs=(rows, P(), rows, P(None, ALL_AXES), P(), P(), rows),
        out_specs=(rows, rows, P()),
        check_vma=False,
    )
```

```python
import functools

import jax
import jax.numpy as jnp
from jax import lax
from jax.experimental import pallas as pl
from jax.experimental.pallas import tpu as pltpu
from jax.sharding import Mesh
from jax.sharding import PartitionSpec as P

F32 = jnp.float32
BF16 = jnp.bfloat16
CHIP_AXES = ("z", "x", "y")
ALL_AXES = ("z", "x", "y", "c")
T = 512
H = 40
PS = 64
N = 128
D = 2560
G = 4
GH = H // G
GL = GH * PS
GT = GL // 128
NM = N // 8
CHIPS = 64
STATE_ROWS = 8 * GT
ROWS = 48
HALF_D = D // 2
GW_ROWS = 40
KC = 5
KL = D // KC
LARGE = 56 << 20
MIDDLE = 44 << 20
SMALL = 10 << 20
WHOLE = pl.BlockSpec(memory_space=pltpu.VMEM)
IN_HBM = pl.BlockSpec(memory_space=pltpu.HBM)
IN_SMEM = pl.BlockSpec(memory_space=pltpu.SMEM)
TOKEN = jax.ShapeDtypeStruct((1,), jnp.int32)


def mm(a, b):
    return jnp.dot(a, b, preferred_element_type=F32)


def mm_nt(a, b):
    return lax.dot_general(a, b, (((1,), (1,)), ((), ())), preferred_element_type=F32)


def mm_tn(a, b):
    return lax.dot_general(a, b, (((0,), (0,)), ((), ())), preferred_element_type=F32)


def spread_matrix():
    k = lax.broadcasted_iota(jnp.int32, (128, GL), 0)
    col = lax.broadcasted_iota(jnp.int32, (128, GL), 1)
    return jnp.where((k & 63) == (col >> 6), 1.0, 0.0).astype(BF16)


def spread(v, onehot):
    high = v.astype(BF16).astype(F32)
    low = pltpu.roll(v - high, 64, 1)
    lane = lax.broadcasted_iota(jnp.int32, v.shape, 1)
    return mm(jnp.where(lane < 64, high, low).astype(BF16), onehot)


def pre_kernel(
    c_ref, rates_ref, hidden_hbm, w_hbm, x_hbm, dy_hbm, codes_hbm,
    bc_hbm, cum_hbm, cumt_hbm, mine_hbm, other_hbm,
    hidden_scr, w_scr, x_scr, dy_scr, codes_scr, bc_scr, cum_scr, cumt_scr, mine_scr, other_scr,
    in_sem, out_sem, small_sem,
):
    is_first = c_ref[0] == 0
    cols = [pl.ds(GL * q, GL) for q in range(G)]
    code_load = pltpu.make_async_copy(codes_hbm, codes_scr, small_sem.at[0])
    code_load.start()
    loads = {}
    for n, (src, dst) in enumerate(((x_hbm, x_scr), (dy_hbm, dy_scr))):
        for q in range(G):
            loads[n, q] = pltpu.make_async_copy(
                src.at[:, cols[q]], dst.at[q], in_sem.at[n, q]
            )
    for q in range(KC):
        part = pl.ds(KL * q, KL)
        loads[2, q] = pltpu.make_async_copy(
            hidden_hbm.at[:, part], hidden_scr.at[q], in_sem.at[2, q]
        )
        loads[3, q] = pltpu.make_async_copy(
            w_hbm.at[part, :], w_scr.at[q], in_sem.at[3, q]
        )
    waves = [(loads[2, q], loads[3, q]) for q in range(KC)]
    waves += [(loads[0, q], loads[1, q]) for q in range(G)]
    ahead = 5

    def take(n):
        for load in waves[n]:
            load.wait()
        if n + ahead < len(waves):
            for load in waves[n + ahead]:
                load.start()

    for wave in waves[:ahead]:
        for load in wave:
            load.start()

    eye = lax.broadcasted_iota(jnp.int32, (H, H), 0) == lax.broadcasted_iota(
        jnp.int32, (H, H), 1
    )
    rates = jnp.sum(jnp.where(eye, rates_ref[...], 0.0), axis=1, keepdims=True)
    s_at = lax.broadcasted_iota(jnp.int32, (T, T), 0)
    t_at = lax.broadcasted_iota(jnp.int32, (T, T), 1)
    upper = jnp.where(s_at <= t_at, 1.0, 0.0).astype(BF16)
    onehot = spread_matrix()
    cum_scr[...] = jnp.zeros_like(cum_scr)
    code_load.wait()
    code = codes_scr[...].astype(F32)
    step = -(
        rates * jnp.minimum(code, 1000.0) / 1000.0
        + 0.0005 * jnp.maximum(code - 1000.0, 0.0)
    )
    p1 = step.astype(BF16)
    rest = step - p1.astype(F32)
    p2 = rest.astype(BF16)
    p3 = (rest - p2.astype(F32)).astype(BF16)
    cum = mm(p1, upper) + mm(p2, upper) + mm(p3, upper)
    stores = []

    def send(src, dst, sem):
        stores.append(pltpu.make_async_copy(src, dst, sem))
        stores[-1].start()

    for q in range(G):
        cum_scr[q, 0:GH, :] = cum[GH * q : GH * (q + 1), :]
        full = jnp.concatenate([cum_scr[q], jnp.zeros((112, T), F32)])
        cumt_scr[q] = full.T
    send(cum_scr, cum_hbm, small_sem.at[1])
    send(cumt_scr, cumt_hbm, small_sem.at[2])
    for q in range(KC):
        take(q)
    depth = [hidden_scr[q] for q in range(KC)]
    acc = mm(jnp.concatenate(depth, axis=1), w_scr[...].reshape(D, 2 * N))
    bc_scr[...] = acc.astype(BF16)
    send(bc_scr, bc_hbm, small_sem.at[3])
    bt = bc_scr[:, :N].T
    ct = bc_scr[:, N:].T
    for q in range(G):
        cumt = cumt_scr[q]
        total = cumt[T - 1 : T, :]
        fw = spread(jnp.exp(cumt), onehot)
        decay = fw[T - 1 : T, :]
        bw = spread(jnp.exp(total - cumt), onehot)
        take(KC + q)
        sf = mm(bt, (x_scr[q].astype(F32) * bw).astype(BF16))
        sb = mm(ct, (dy_scr[q].astype(F32) * fw).astype(BF16))
        rows = pl.ds(NM * q, NM)
        for n, (scr, hbm, state) in enumerate(
            (
                (other_scr, other_hbm, jnp.where(is_first, sb, sf)),
                (mine_scr, mine_hbm, jnp.where(is_first, sf, sb)),
            )
        ):
            for m in range(NM):
                for i in range(GT):
                    lanes = slice(128 * i, 128 * i + 128)
                    scr[NM * q + m, 8 * i : 8 * i + 8, :] = state[8 * m : 8 * m + 8, lanes]
                    row = STATE_ROWS + i
                    scr[NM * q + m, row : row + 1, :] = decay[:, lanes]
                scr[NM * q + m, STATE_ROWS + GT : ROWS, :] = jnp.zeros(
                    (ROWS - STATE_ROWS - GT, 128), F32
                )
            send(scr.at[rows], hbm.at[rows], out_sem.at[n, q])
    for store in stores:
        store.wait()


def pre(core, hidden, w_bc, x, dy, codes, rates):
    return pl.pallas_call(
        pre_kernel,
        in_specs=[pl.BlockSpec(memory_space=pltpu.SMEM), WHOLE] + [IN_HBM] * 5,
        out_specs=[IN_HBM] * 5,
        out_shape=[
            jax.ShapeDtypeStruct((T, 2 * N), BF16),
            jax.ShapeDtypeStruct((G, 16, T), F32),
            jax.ShapeDtypeStruct((G, T, 128), F32),
            jax.ShapeDtypeStruct((CHIPS, ROWS, 128), F32),
            jax.ShapeDtypeStruct((CHIPS, ROWS, 128), F32),
        ],
        scratch_shapes=[
            pltpu.VMEM((KC, T, KL), BF16),
            pltpu.VMEM((KC, KL, 2 * N), BF16),
            pltpu.VMEM((G, T, GL), BF16),
            pltpu.VMEM((G, T, GL), BF16),
            pltpu.VMEM((H, T), jnp.int32),
            pltpu.VMEM((T, 2 * N), BF16),
            pltpu.VMEM((G, 16, T), F32),
            pltpu.VMEM((G, T, 128), F32),
            pltpu.VMEM((CHIPS, ROWS, 128), F32),
            pltpu.VMEM((CHIPS, ROWS, 128), F32),
            pltpu.SemaphoreType.DMA((4, KC)),
            pltpu.SemaphoreType.DMA((2, G)),
            pltpu.SemaphoreType.DMA((4,)),
        ],
        compiler_params=pltpu.CompilerParams(vmem_limit_bytes=LARGE),
        cost_estimate=pl.CostEstimate(
            flops=2 * 10**9, bytes_accessed=13 * 10**6, transcendentals=0
        ),
        name="pre",
    )(core, rates, hidden, w_bc, x, dy, codes)


def chip_kernel(mine_ref, got_ref, out_ref):
    for m in range(CHIPS):
        for i in range(GT):
            other = got_ref[m, STATE_ROWS + i : STATE_ROWS + i + 1, :]
            rows = slice(8 * i, 8 * i + 8)
            out_ref[m, rows, :] = other * mine_ref[m, rows, :] + got_ref[m, rows, :]
        tail = slice(STATE_ROWS, ROWS)
        out_ref[m, tail, :] = mine_ref[m, tail, :] * got_ref[m, tail, :]


def chip_sum(mine, got):
    return pl.pallas_call(
        chip_kernel,
        in_specs=[WHOLE, WHOLE],
        out_specs=WHOLE,
        out_shape=jax.ShapeDtypeStruct((CHIPS, ROWS, 128), F32),
        compiler_params=pltpu.CompilerParams(vmem_limit_bytes=SMALL),
        name="chip_sum",
    )(mine, got)


def scan_kernel(c_ref, in_ref, after_ref, out_ref):
    core = c_ref[0]
    state = [jnp.zeros((8, 128), F32) for _ in range(GT)]
    for k in range(CHIPS):
        at = k + core * (CHIPS - 1 - 2 * k)
        for i in range(GT):
            rows = slice(8 * i, 8 * i + 8)
            out_ref[at, rows, :] = state[i]
            decay = in_ref[at, STATE_ROWS + i : STATE_ROWS + i + 1, :]
            state[i] = decay * state[i] + in_ref[at, rows, :]


def scan_chips(core, slices, after):
    return pl.pallas_call(
        scan_kernel,
        in_specs=[IN_SMEM, WHOLE, IN_SMEM],
        out_specs=WHOLE,
        out_shape=jax.ShapeDtypeStruct((CHIPS, STATE_ROWS, 128), F32),
        compiler_params=pltpu.CompilerParams(vmem_limit_bytes=SMALL),
        name="scan_chips",
    )(core, slices, after)


SPANS = ((0, 256), (0, 128), (256, 128))
CHUNK = 128


def span_weights(cumt, onehot, start, size):
    lo = slice(start, start + size)
    hi = slice(start + size, start + 2 * size)
    edge = cumt[start + size - 1 : start + size, :]
    u_lo = spread(jnp.exp(edge - cumt[lo, :]), onehot)
    u_hi = spread(jnp.exp(cumt[hi, :] - edge), onehot)
    return lo, hi, u_lo, u_hi


def chunk_masks():
    t_at = lax.broadcasted_iota(jnp.int32, (CHUNK, CHUNK), 0)
    s_at = lax.broadcasted_iota(jnp.int32, (CHUNK, CHUNK), 1)
    return t_at >= s_at, s_at < PS


def chunk_decay(cumt, cum_ref, rows, h, lower):
    gap = cumt[rows, h : h + 1] - cum_ref[0, h : h + 1, rows]
    return jnp.exp(jnp.where(lower, gap, -jnp.inf))


def pairs_kernel(
    c_ref, bc_ref, x_ref, dy_ref, cum_ref, cumt_ref, hidden_ref, after_ref,
    wmine_ref, wother_ref, dbc_ref, turned_ref, token_ref, kmat,
):
    q = pl.program_id(0)
    is_first = c_ref[0] == 0

    @pl.when(q == 0)
    def _():
        kmat[...] = jnp.zeros_like(kmat)

    turned_ref[...] = hidden_ref[...].T
    onehot = spread_matrix()
    cumt = cumt_ref[0]
    x = x_ref[...].astype(F32)
    dy = dy_ref[...].astype(F32)
    wg = dy * spread(jnp.exp(cumt), onehot)
    wi = x * spread(jnp.exp(cumt[T - 1 : T, :] - cumt), onehot)
    wmine_ref[...] = jnp.where(is_first, wg, wi).astype(BF16)
    wother_ref[...] = jnp.where(is_first, wi, wg).astype(BF16)
    for start, size in SPANS:
        lo, hi, u_lo, u_hi = span_weights(cumt, onehot, start, size)
        kmat[hi, lo] += mm_nt((dy[hi, :] * u_hi).astype(BF16), (x[lo, :] * u_lo).astype(BF16))
    lower, first = chunk_masks()
    for chunk in range(T // CHUNK):
        rows = slice(chunk * CHUNK, (chunk + 1) * CHUNK)
        ksum = jnp.zeros((CHUNK, CHUNK), F32)
        for i in range(GT):
            lanes = slice(128 * i, 128 * i + 128)
            xt = x_ref[rows, lanes]
            dyf = dy[rows, lanes]
            for e in range(2):
                own = first if e == 0 else jnp.logical_not(first)
                dyh = jnp.where(own, dyf, 0.0).astype(BF16)
                ksum += chunk_decay(cumt, cum_ref, rows, 2 * i + e, lower) * mm_nt(dyh, xt)
        kmat[rows, rows] += ksum

    @pl.when(q == G - 1)
    def _():
        k = kmat[...].astype(BF16)
        dbc_ref[:, :N] = mm_tn(k, bc_ref[:, N:])
        dbc_ref[:, N:] = mm(k, bc_ref[:, :N])
        token_ref[0] = 0


def full_spec(*shape):
    return pl.BlockSpec(shape, lambda q: (0,) * len(shape))


def cols_spec(rows=T):
    return pl.BlockSpec((rows, GL), lambda q: (0, q))


def group_spec(*shape):
    return pl.BlockSpec((1, *shape), lambda q: (q, 0, 0))


def pairs(core, bc, x, dy, cum, cumt, hidden, after):
    return pl.pallas_call(
        pairs_kernel,
        grid=(G,),
        in_specs=[
            pl.BlockSpec(memory_space=pltpu.SMEM),
            full_spec(T, 2 * N),
            cols_spec(),
            cols_spec(),
            group_spec(16, T),
            group_spec(T, 128),
            cols_spec(),
            IN_HBM,
        ],
        out_specs=[
            cols_spec(),
            cols_spec(),
            full_spec(T, 2 * N),
            pl.BlockSpec((GL, T), lambda q: (q, 0)),
            IN_SMEM,
        ],
        out_shape=[
            jax.ShapeDtypeStruct((T, D), BF16),
            jax.ShapeDtypeStruct((T, D), BF16),
            jax.ShapeDtypeStruct((T, 2 * N), F32),
            jax.ShapeDtypeStruct((D, T), BF16),
            TOKEN,
        ],
        scratch_shapes=[pltpu.VMEM((T, T), F32)],
        compiler_params=pltpu.CompilerParams(vmem_limit_bytes=LARGE),
        cost_estimate=pl.CostEstimate(
            flops=20 * 10**9, bytes_accessed=16 * 10**6, transcendentals=3 * 10**6
        ),
        name="pairs",
    )(core, bc, x, dy, cum, cumt, hidden, after)


def carry_kernel(w_ref, came_ref, acc_ref, state_ref):
    acc = jnp.zeros((T, N), F32)
    for q in range(G):
        for i in range(GT):
            rows = slice(8 * i, 8 * i + 8)
            lanes = slice(GL * q + 128 * i, GL * q + 128 * i + 128)
            for m in range(0, NM, 2):
                at = NM * q + m
                pair = jnp.concatenate([came_ref[at, rows, :], came_ref[at + 1, rows, :]])
                state_ref[8 * m : 8 * m + 16, lanes] = pair.astype(BF16)
        cols = slice(GL * q, GL * (q + 1))
        acc += mm_nt(w_ref[:, cols], state_ref[:, cols])
    acc_ref[...] = acc


def carry(w_mine, came):
    return pl.pallas_call(
        carry_kernel,
        in_specs=[WHOLE, WHOLE],
        out_specs=[WHOLE, WHOLE],
        out_shape=[
            jax.ShapeDtypeStruct((T, N), F32),
            jax.ShapeDtypeStruct((N, D), BF16),
        ],
        compiler_params=pltpu.CompilerParams(vmem_limit_bytes=SMALL),
        cost_estimate=pl.CostEstimate(
            flops=4 * 10**8, bytes_accessed=5 * 10**6, transcendentals=0
        ),
        name="carry",
    )(w_mine, came)


def weight_kernel(
    c_ref, accmine_ref, wother_ref, came_ref, theirs_ref, dbc_ref, turned_hbm,
    gwmine_ref, gwother_ref, state_ref, turned_scr, sem,
):
    core = c_ref[0]
    is_first = core == 0
    starts = [pl.multiple_of(half * HALF_D, HALF_D) for half in (1 - core, core)]
    loads = [
        pltpu.make_async_copy(
            turned_hbm.at[pl.ds(start, HALF_D), :], turned_scr.at[n], sem.at[n]
        )
        for n, start in enumerate(starts)
    ]
    for load in loads:
        load.start()
    acc = jnp.zeros((T, N), F32)
    for q in range(G):
        for i in range(GT):
            rows = slice(8 * i, 8 * i + 8)
            lanes = slice(GL * q + 128 * i, GL * q + 128 * i + 128)
            tail = slice(STATE_ROWS + i, STATE_ROWS + i + 1)
            decay = theirs_ref[NM * q, tail, :]
            for m in range(0, NM, 2):
                at = NM * q + m
                pair = jnp.concatenate(
                    [
                        decay * came_ref[k, rows, :] + theirs_ref[k, rows, :]
                        for k in (at, at + 1)
                    ]
                )
                state_ref[8 * m : 8 * m + 16, lanes] = pair.astype(BF16)
        cols = slice(GL * q, GL * (q + 1))
        acc += mm_nt(wother_ref[:, cols], state_ref[:, cols])
    mine = accmine_ref[...]
    db = dbc_ref[:, :N] + jnp.where(is_first, acc, mine)
    dc = dbc_ref[:, N:] + jnp.where(is_first, mine, acc)
    dbc = (jnp.concatenate([db, dc], axis=1) * (1.0 / (T * 2 * CHIPS))).astype(BF16)
    for n, ref in enumerate((gwother_ref, gwmine_ref)):
        loads[n].wait()
        part = mm(turned_scr[n], dbc)
        ref[0] = part[:, :N]
        ref[1] = part[:, N:]


def weight_part(core, acc_mine, w_other, came, theirs, dbc, turned):
    return pl.pallas_call(
        weight_kernel,
        in_specs=[IN_SMEM] + [WHOLE] * 5 + [IN_HBM],
        out_specs=[WHOLE, WHOLE, WHOLE],
        out_shape=[
            jax.ShapeDtypeStruct((2, HALF_D, N), F32),
            jax.ShapeDtypeStruct((2, HALF_D, N), F32),
            jax.ShapeDtypeStruct((N, D), BF16),
        ],
        scratch_shapes=[
            pltpu.VMEM((2, HALF_D, T), BF16),
            pltpu.SemaphoreType.DMA((2,)),
        ],
        compiler_params=pltpu.CompilerParams(vmem_limit_bytes=MIDDLE),
        cost_estimate=pl.CostEstimate(
            flops=2 * 10**9, bytes_accessed=12 * 10**6, transcendentals=0
        ),
        name="weight_part",
    )(core, acc_mine, w_other, came, theirs, dbc, turned)


def outputs_kernel(
    c_ref, bc_ref, x_ref, dy_ref, cum_ref, cumt_ref, skip_ref, smine_ref, sother_ref, after_ref,
    mixed_ref, gradx_ref, token_ref, scores, yacc, dxacc,
):
    is_first = c_ref[0] == 0
    b_mat = bc_ref[:, :N]
    c_mat = bc_ref[:, N:]

    @pl.when(pl.program_id(0) == 0)
    def _():
        scores[...] = mm_nt(c_mat, b_mat)

    onehot = spread_matrix()
    cumt = cumt_ref[0]
    x = x_ref[...].astype(F32)
    dy = dy_ref[...].astype(F32)
    skip = skip_ref[...]
    mine = smine_ref[...].astype(F32)
    other = sother_ref[...].astype(F32)
    s_prev = jnp.where(is_first, mine, other).astype(BF16)
    g_next = jnp.where(is_first, other, mine).astype(BF16)
    fw = spread(jnp.exp(cumt), onehot)
    yacc[...] = skip * x + fw * mm(c_mat, s_prev)
    bw = spread(jnp.exp(cumt[T - 1 : T, :] - cumt), onehot)
    dxacc[...] = skip * dy + bw * mm(b_mat, g_next)
    for start, size in SPANS:
        lo, hi, u_lo, u_hi = span_weights(cumt, onehot, start, size)
        pair = scores[hi, lo].astype(BF16)
        yacc[hi, :] += u_hi * mm(pair, (x[lo, :] * u_lo).astype(BF16))
        dxacc[lo, :] += u_lo * mm_tn(pair, (dy[hi, :] * u_hi).astype(BF16))
    lower, first = chunk_masks()
    for chunk in range(T // CHUNK):
        rows = slice(chunk * CHUNK, (chunk + 1) * CHUNK)
        score = scores[rows, rows]
        for i in range(GT):
            lanes = slice(128 * i, 128 * i + 128)
            xt = x_ref[rows, lanes]
            dyt = dy_ref[rows, lanes]
            ys, dxs = [], []
            for e in range(2):
                decay = chunk_decay(cumt, cum_ref, rows, 2 * i + e, lower)
                mixing = (score * decay).astype(BF16)
                ys.append(mm(mixing, xt))
                dxs.append(mm_tn(mixing, dyt))
            mixed_ref[rows, lanes] = (
                yacc[rows, lanes] + jnp.where(first, ys[0], ys[1])
            ).astype(BF16)
            gradx_ref[rows, lanes] = (
                dxacc[rows, lanes] + jnp.where(first, dxs[0], dxs[1])
            ).astype(BF16)
    token_ref[0] = 0


def outputs(core, bc, x, dy, cum, cumt, skip_row, s_mine, s_other, after):
    return pl.pallas_call(
        outputs_kernel,
        grid=(G,),
        in_specs=[
            pl.BlockSpec(memory_space=pltpu.SMEM),
            full_spec(T, 2 * N),
            cols_spec(),
            cols_spec(),
            group_spec(16, T),
            group_spec(T, 128),
            cols_spec(1),
            cols_spec(N),
            cols_spec(N),
            IN_HBM,
        ],
        out_specs=[cols_spec(), cols_spec(), IN_SMEM],
        out_shape=[
            jax.ShapeDtypeStruct((T, D), BF16),
            jax.ShapeDtypeStruct((T, D), BF16),
            TOKEN,
        ],
        scratch_shapes=[
            pltpu.VMEM((T, T), F32),
            pltpu.VMEM((T, GL), F32),
            pltpu.VMEM((T, GL), F32),
        ],
        compiler_params=pltpu.CompilerParams(vmem_limit_bytes=LARGE),
        cost_estimate=pl.CostEstimate(
            flops=25 * 10**9, bytes_accessed=13 * 10**6, transcendentals=3 * 10**6
        ),
        name="outputs",
    )(core, bc, x, dy, cum, cumt, skip_row, s_mine, s_other, after)


def add_kernel(a_ref, b_ref, out_hbm, scr, sem):
    block = HALF_D // 2
    stores = []
    for lane in range(2):
        for i in range(2):
            rows = pl.ds(block * i, block)
            scr[lane, rows, :] = a_ref[lane, rows, :] + b_ref[lane, rows, :]
            stores.append(
                pltpu.make_async_copy(
                    scr.at[lane, rows], out_hbm.at[lane, rows], sem.at[lane, i]
                )
            )
            stores[-1].start()
    for store in stores:
        store.wait()


def pair_add(a, b):
    return pl.pallas_call(
        add_kernel,
        in_specs=[WHOLE, WHOLE],
        out_specs=IN_HBM,
        out_shape=jax.ShapeDtypeStruct(a.shape, F32),
        scratch_shapes=[
            pltpu.VMEM(a.shape, F32),
            pltpu.SemaphoreType.DMA((2, 2)),
        ],
        compiler_params=pltpu.CompilerParams(vmem_limit_bytes=MIDDLE),
        name="pair_add",
    )(a, b)


def total_kernel(in_ref, after_ref, out_ref):
    total = jnp.sum(in_ref[...], axis=0)
    for k in range(CHIPS):
        out_ref[k] = total


def chip_total(parts, after):
    return pl.pallas_call(
        total_kernel,
        in_specs=[WHOLE, IN_SMEM],
        out_specs=WHOLE,
        out_shape=jax.ShapeDtypeStruct((CHIPS, GW_ROWS, 128), F32),
        compiler_params=pltpu.CompilerParams(vmem_limit_bytes=SMALL),
        name="chip_total",
    )(parts, after)


def place_kernel(c_ref, half_ref, *refs):
    out_ref = refs[-1]
    for lane in range(2):
        out_ref[:, 128 * lane : 128 * lane + 128] = half_ref[lane]


def place(at, half, into):
    block = HALF_D // 2
    extra = [] if into is None else [into]
    return pl.pallas_call(
        place_kernel,
        grid_spec=pltpu.PrefetchScalarGridSpec(
            num_scalar_prefetch=1,
            grid=(2,),
            in_specs=[pl.BlockSpec((2, block, 128), lambda i, c: (0, i, 0))]
            + [pl.BlockSpec(memory_space=pl.ANY)] * len(extra),
            out_specs=pl.BlockSpec((block, 2 * N), lambda i, c: (2 * c[0] + i, 0)),
        ),
        out_shape=jax.ShapeDtypeStruct((D, 2 * N), F32),
        input_output_aliases={2: 0} if extra else {},
        compiler_params=pltpu.CompilerParams(vmem_limit_bytes=SMALL),
        name="place",
    )(at, half, *extra)


def swap(v):
    return lax.ppermute(v, "c", [(0, 1), (1, 0)])


def exchange(v):
    return lax.all_to_all(v, CHIP_AXES, 0, 0, tiled=True)


def shards(hidden, w_bc, ssm_in, codes, rates, skip, grad_out):
    core = lax.axis_index("c").astype(jnp.int32).reshape(1)
    skip_row = jnp.repeat(skip, PS)[None, :]
    bc, cum, cumt, mine, other = pre(
        core, hidden, w_bc, ssm_in, grad_out, codes, rates[None, :]
    )
    chip = chip_sum(mine, swap(other))
    slices = exchange(chip)
    theirs = swap(mine)
    w_mine, w_other, dbc, turned, paired = pairs(
        core, bc, ssm_in, grad_out, cum, cumt, hidden, chip
    )
    came = exchange(scan_chips(core, slices, paired))
    acc_mine, s_mine = carry(w_mine, came)
    gw_mine, gw_other, s_other = weight_part(
        core, acc_mine, w_other, swap(came), theirs, dbc, turned
    )
    part = pair_add(gw_mine, swap(gw_other))
    sums = exchange(part.reshape(CHIPS, GW_ROWS, 128))
    mixed, gradx, done = outputs(
        core, bc, ssm_in, grad_out, cum, cumt, skip_row, s_mine, s_other, part
    )
    half = exchange(chip_total(sums, done)).reshape(2, HALF_D, 128)
    grad_w = place(1 - core, swap(half), place(core, half, None))
    return mixed, gradx, grad_w


def solution(mesh):
    grid = Mesh(mesh.devices.reshape(4, 4, 4, 2), ALL_AXES)
    rows = P(ALL_AXES, None)
    return jax.shard_map(
        shards,
        mesh=grid,
        in_specs=(rows, P(), rows, P(None, ALL_AXES), P(), P(), rows),
        out_specs=(rows, rows, P()),
        check_vma=False,
    )
```

```python
import functools

import jax
import jax.numpy as jnp
from jax import lax
from jax.experimental import pallas as pl
from jax.experimental.pallas import tpu as pltpu
from jax.sharding import Mesh
from jax.sharding import PartitionSpec as P

F32 = jnp.float32
BF16 = jnp.bfloat16
CHIP_AXES = ("z", "x", "y")
ALL_AXES = ("z", "x", "y", "c")
T = 512
H = 40
PS = 64
N = 128
D = 2560
G = 4
GH = H // G
GL = GH * PS
GT = GL // 128
NM = N // 8
CHIPS = 64
STATE_ROWS = 8 * GT
ROWS = 48
HALF_D = D // 2
PLANE = 16
GW_ROWS = 2 * HALF_D // PLANE
KC = 5
KL = D // KC
LARGE = 56 << 20
MIDDLE = 44 << 20
SMALL = 10 << 20
WHOLE = pl.BlockSpec(memory_space=pltpu.VMEM)
IN_HBM = pl.BlockSpec(memory_space=pltpu.HBM)
IN_SMEM = pl.BlockSpec(memory_space=pltpu.SMEM)
TOKEN = jax.ShapeDtypeStruct((1,), jnp.int32)


def mm(a, b):
    return jnp.dot(a, b, preferred_element_type=F32)


def mm_nt(a, b):
    return lax.dot_general(a, b, (((1,), (1,)), ((), ())), preferred_element_type=F32)


def mm_tn(a, b):
    return lax.dot_general(a, b, (((0,), (0,)), ((), ())), preferred_element_type=F32)


def spread_matrix():
    k = lax.broadcasted_iota(jnp.int32, (128, GL), 0)
    col = lax.broadcasted_iota(jnp.int32, (128, GL), 1)
    return jnp.where((k & 63) == (col >> 6), 1.0, 0.0).astype(BF16)


def spread(v, onehot):
    high = v.astype(BF16).astype(F32)
    low = pltpu.roll(v - high, 64, 1)
    lane = lax.broadcasted_iota(jnp.int32, v.shape, 1)
    return mm(jnp.where(lane < 64, high, low).astype(BF16), onehot)


def pre_kernel(
    c_ref, rates_ref, hidden_hbm, w_hbm, x_hbm, dy_hbm, codes_hbm,
    bc_hbm, cum_hbm, cumt_hbm, mine_hbm, other_hbm,
    hidden_scr, w_scr, x_scr, dy_scr, codes_scr, bc_scr, cum_scr, cumt_scr, mine_scr, other_scr,
    in_sem, out_sem, small_sem,
):
    is_first = c_ref[0] == 0
    cols = [pl.ds(GL * q, GL) for q in range(G)]
    code_load = pltpu.make_async_copy(codes_hbm, codes_scr, small_sem.at[0])
    code_load.start()
    loads = {}
    for n, (src, dst) in enumerate(((x_hbm, x_scr), (dy_hbm, dy_scr))):
        for q in range(G):
            loads[n, q] = pltpu.make_async_copy(
                src.at[:, cols[q]], dst.at[q], in_sem.at[n, q]
            )
    for q in range(KC):
        part = pl.ds(KL * q, KL)
        loads[2, q] = pltpu.make_async_copy(
            hidden_hbm.at[:, part], hidden_scr.at[q], in_sem.at[2, q]
        )
        loads[3, q] = pltpu.make_async_copy(
            w_hbm.at[part, :], w_scr.at[q], in_sem.at[3, q]
        )
    waves = [(loads[2, q], loads[3, q]) for q in range(KC)]
    waves += [(loads[0, q], loads[1, q]) for q in range(G)]
    ahead = 5

    def take(n):
        for load in waves[n]:
            load.wait()
        if n + ahead < len(waves):
            for load in waves[n + ahead]:
                load.start()

    for wave in waves[:ahead]:
        for load in wave:
            load.start()

    eye = lax.broadcasted_iota(jnp.int32, (H, H), 0) == lax.broadcasted_iota(
        jnp.int32, (H, H), 1
    )
    rates = jnp.sum(jnp.where(eye, rates_ref[...], 0.0), axis=1, keepdims=True)
    s_at = lax.broadcasted_iota(jnp.int32, (T, T), 0)
    t_at = lax.broadcasted_iota(jnp.int32, (T, T), 1)
    upper = jnp.where(s_at <= t_at, 1.0, 0.0).astype(BF16)
    onehot = spread_matrix()
    cum_scr[...] = jnp.zeros_like(cum_scr)
    code_load.wait()
    code = codes_scr[...].astype(F32)
    step = -(
        rates * jnp.minimum(code, 1000.0) / 1000.0
        + 0.0005 * jnp.maximum(code - 1000.0, 0.0)
    )
    p1 = step.astype(BF16)
    rest = step - p1.astype(F32)
    p2 = rest.astype(BF16)
    p3 = (rest - p2.astype(F32)).astype(BF16)
    cum = mm(p1, upper) + mm(p2, upper) + mm(p3, upper)
    stores = []

    def send(src, dst, sem):
        stores.append(pltpu.make_async_copy(src, dst, sem))
        stores[-1].start()

    for q in range(G):
        cum_scr[q, 0:GH, :] = cum[GH * q : GH * (q + 1), :]
        full = jnp.concatenate([cum_scr[q], jnp.zeros((112, T), F32)])
        cumt_scr[q] = full.T
    send(cum_scr, cum_hbm, small_sem.at[1])
    send(cumt_scr, cumt_hbm, small_sem.at[2])
    for q in range(KC):
        take(q)
    depth = [hidden_scr[q] for q in range(KC)]
    acc = mm(jnp.concatenate(depth, axis=1), w_scr[...].reshape(D, 2 * N))
    bc_scr[...] = acc.astype(BF16)
    send(bc_scr, bc_hbm, small_sem.at[3])
    bt = bc_scr[:, :N].T
    ct = bc_scr[:, N:].T
    for q in range(G):
        cumt = cumt_scr[q]
        total = cumt[T - 1 : T, :]
        fw = spread(jnp.exp(cumt), onehot)
        decay = fw[T - 1 : T, :]
        bw = spread(jnp.exp(total - cumt), onehot)
        take(KC + q)
        sf = mm(bt, (x_scr[q].astype(F32) * bw).astype(BF16))
        sb = mm(ct, (dy_scr[q].astype(F32) * fw).astype(BF16))
        rows = pl.ds(NM * q, NM)
        for n, (scr, hbm, state) in enumerate(
            (
                (other_scr, other_hbm, jnp.where(is_first, sb, sf)),
                (mine_scr, mine_hbm, jnp.where(is_first, sf, sb)),
            )
        ):
            for m in range(NM):
                for i in range(GT):
                    lanes = slice(128 * i, 128 * i + 128)
                    scr[NM * q + m, 8 * i : 8 * i + 8, :] = state[8 * m : 8 * m + 8, lanes]
                    row = STATE_ROWS + i
                    scr[NM * q + m, row : row + 1, :] = decay[:, lanes]
                scr[NM * q + m, STATE_ROWS + GT : ROWS, :] = jnp.zeros(
                    (ROWS - STATE_ROWS - GT, 128), F32
                )
            send(scr.at[rows], hbm.at[rows], out_sem.at[n, q])
    for store in stores:
        store.wait()


def pre(core, hidden, w_bc, x, dy, codes, rates):
    return pl.pallas_call(
        pre_kernel,
        in_specs=[pl.BlockSpec(memory_space=pltpu.SMEM), WHOLE] + [IN_HBM] * 5,
        out_specs=[IN_HBM] * 5,
        out_shape=[
            jax.ShapeDtypeStruct((T, 2 * N), BF16),
            jax.ShapeDtypeStruct((G, 16, T), F32),
            jax.ShapeDtypeStruct((G, T, 128), F32),
            jax.ShapeDtypeStruct((CHIPS, ROWS, 128), F32),
            jax.ShapeDtypeStruct((CHIPS, ROWS, 128), F32),
        ],
        scratch_shapes=[
            pltpu.VMEM((KC, T, KL), BF16),
            pltpu.VMEM((KC, KL, 2 * N), BF16),
            pltpu.VMEM((G, T, GL), BF16),
            pltpu.VMEM((G, T, GL), BF16),
            pltpu.VMEM((H, T), jnp.int32),
            pltpu.VMEM((T, 2 * N), BF16),
            pltpu.VMEM((G, 16, T), F32),
            pltpu.VMEM((G, T, 128), F32),
            pltpu.VMEM((CHIPS, ROWS, 128), F32),
            pltpu.VMEM((CHIPS, ROWS, 128), F32),
            pltpu.SemaphoreType.DMA((4, KC)),
            pltpu.SemaphoreType.DMA((2, G)),
            pltpu.SemaphoreType.DMA((4,)),
        ],
        compiler_params=pltpu.CompilerParams(vmem_limit_bytes=LARGE),
        cost_estimate=pl.CostEstimate(
            flops=2 * 10**9, bytes_accessed=13 * 10**6, transcendentals=0
        ),
        name="pre",
    )(core, rates, hidden, w_bc, x, dy, codes)


def chip_kernel(mine_ref, got_ref, out_ref):
    for m in range(CHIPS):
        for i in range(GT):
            other = got_ref[m, STATE_ROWS + i : STATE_ROWS + i + 1, :]
            rows = slice(8 * i, 8 * i + 8)
            out_ref[m, rows, :] = other * mine_ref[m, rows, :] + got_ref[m, rows, :]
        tail = slice(STATE_ROWS, ROWS)
        out_ref[m, tail, :] = mine_ref[m, tail, :] * got_ref[m, tail, :]


def chip_sum(mine, got):
    return pl.pallas_call(
        chip_kernel,
        in_specs=[WHOLE, WHOLE],
        out_specs=WHOLE,
        out_shape=jax.ShapeDtypeStruct((CHIPS, ROWS, 128), F32),
        compiler_params=pltpu.CompilerParams(vmem_limit_bytes=SMALL),
        name="chip_sum",
    )(mine, got)


def scan_kernel(c_ref, in_ref, after_ref, out_ref):
    core = c_ref[0]
    state = [jnp.zeros((8, 128), F32) for _ in range(GT)]
    for k in range(CHIPS):
        at = k + core * (CHIPS - 1 - 2 * k)
        for i in range(GT):
            rows = slice(8 * i, 8 * i + 8)
            out_ref[at, rows, :] = state[i]
            decay = in_ref[at, STATE_ROWS + i : STATE_ROWS + i + 1, :]
            state[i] = decay * state[i] + in_ref[at, rows, :]


def scan_chips(core, slices, after):
    return pl.pallas_call(
        scan_kernel,
        in_specs=[IN_SMEM, WHOLE, IN_SMEM],
        out_specs=WHOLE,
        out_shape=jax.ShapeDtypeStruct((CHIPS, STATE_ROWS, 128), F32),
        compiler_params=pltpu.CompilerParams(vmem_limit_bytes=SMALL),
        name="scan_chips",
    )(core, slices, after)


SPANS = ((0, 256), (0, 128), (256, 128))
CHUNK = 128


def span_weights(cumt, onehot, start, size):
    lo = slice(start, start + size)
    hi = slice(start + size, start + 2 * size)
    edge = cumt[start + size - 1 : start + size, :]
    u_lo = spread(jnp.exp(edge - cumt[lo, :]), onehot)
    u_hi = spread(jnp.exp(cumt[hi, :] - edge), onehot)
    return lo, hi, u_lo, u_hi


def chunk_masks():
    t_at = lax.broadcasted_iota(jnp.int32, (CHUNK, CHUNK), 0)
    s_at = lax.broadcasted_iota(jnp.int32, (CHUNK, CHUNK), 1)
    return t_at >= s_at, s_at < PS


def chunk_decay(cumt, cum_ref, rows, h, lower):
    gap = cumt[rows, h : h + 1] - cum_ref[0, h : h + 1, rows]
    return jnp.exp(jnp.where(lower, gap, -jnp.inf))


def pairs_kernel(
    c_ref, bc_ref, x_ref, dy_ref, cum_ref, cumt_ref, hidden_ref, after_ref,
    wmine_ref, wother_ref, dbc_ref, turned_ref, token_ref, kmat,
):
    q = pl.program_id(0)
    is_first = c_ref[0] == 0

    @pl.when(q == 0)
    def _():
        kmat[...] = jnp.zeros_like(kmat)

    turned_ref[...] = hidden_ref[...].T
    onehot = spread_matrix()
    cumt = cumt_ref[0]
    x = x_ref[...].astype(F32)
    dy = dy_ref[...].astype(F32)
    wg = dy * spread(jnp.exp(cumt), onehot)
    wi = x * spread(jnp.exp(cumt[T - 1 : T, :] - cumt), onehot)
    wmine_ref[...] = jnp.where(is_first, wg, wi).astype(BF16)
    wother_ref[...] = jnp.where(is_first, wi, wg).astype(BF16)
    for start, size in SPANS:
        lo, hi, u_lo, u_hi = span_weights(cumt, onehot, start, size)
        kmat[hi, lo] += mm_nt((dy[hi, :] * u_hi).astype(BF16), (x[lo, :] * u_lo).astype(BF16))
    lower, first = chunk_masks()
    for chunk in range(T // CHUNK):
        rows = slice(chunk * CHUNK, (chunk + 1) * CHUNK)
        ksum = jnp.zeros((CHUNK, CHUNK), F32)
        for i in range(GT):
            lanes = slice(128 * i, 128 * i + 128)
            xt = x_ref[rows, lanes]
            dyf = dy[rows, lanes]
            for e in range(2):
                own = first if e == 0 else jnp.logical_not(first)
                dyh = jnp.where(own, dyf, 0.0).astype(BF16)
                ksum += chunk_decay(cumt, cum_ref, rows, 2 * i + e, lower) * mm_nt(dyh, xt)
        kmat[rows, rows] += ksum

    @pl.when(q == G - 1)
    def _():
        k = kmat[...].astype(BF16)
        dbc_ref[:, :N] = mm_tn(k, bc_ref[:, N:])
        dbc_ref[:, N:] = mm(k, bc_ref[:, :N])
        token_ref[0] = 0


def full_spec(*shape):
    return pl.BlockSpec(shape, lambda q: (0,) * len(shape))


def cols_spec(rows=T):
    return pl.BlockSpec((rows, GL), lambda q: (0, q))


def group_spec(*shape):
    return pl.BlockSpec((1, *shape), lambda q: (q, 0, 0))


def pairs(core, bc, x, dy, cum, cumt, hidden, after):
    return pl.pallas_call(
        pairs_kernel,
        grid=(G,),
        in_specs=[
            pl.BlockSpec(memory_space=pltpu.SMEM),
            full_spec(T, 2 * N),
            cols_spec(),
            cols_spec(),
            group_spec(16, T),
            group_spec(T, 128),
            cols_spec(),
            IN_HBM,
        ],
        out_specs=[
            cols_spec(),
            cols_spec(),
            full_spec(T, 2 * N),
            pl.BlockSpec((GL, T), lambda q: (q, 0)),
            IN_SMEM,
        ],
        out_shape=[
            jax.ShapeDtypeStruct((T, D), BF16),
            jax.ShapeDtypeStruct((T, D), BF16),
            jax.ShapeDtypeStruct((T, 2 * N), F32),
            jax.ShapeDtypeStruct((D, T), BF16),
            TOKEN,
        ],
        scratch_shapes=[pltpu.VMEM((T, T), F32)],
        compiler_params=pltpu.CompilerParams(vmem_limit_bytes=LARGE),
        cost_estimate=pl.CostEstimate(
            flops=20 * 10**9, bytes_accessed=16 * 10**6, transcendentals=3 * 10**6
        ),
        name="pairs",
    )(core, bc, x, dy, cum, cumt, hidden, after)


def carry_kernel(w_ref, came_ref, acc_ref, state_ref):
    acc = jnp.zeros((T, N), F32)
    for q in range(G):
        for i in range(GT):
            rows = slice(8 * i, 8 * i + 8)
            lanes = slice(GL * q + 128 * i, GL * q + 128 * i + 128)
            for m in range(0, NM, 2):
                at = NM * q + m
                pair = jnp.concatenate([came_ref[at, rows, :], came_ref[at + 1, rows, :]])
                state_ref[8 * m : 8 * m + 16, lanes] = pair.astype(BF16)
        cols = slice(GL * q, GL * (q + 1))
        acc += mm_nt(w_ref[:, cols], state_ref[:, cols])
    acc_ref[...] = acc


def carry(w_mine, came):
    return pl.pallas_call(
        carry_kernel,
        in_specs=[WHOLE, WHOLE],
        out_specs=[WHOLE, WHOLE],
        out_shape=[
            jax.ShapeDtypeStruct((T, N), F32),
            jax.ShapeDtypeStruct((N, D), BF16),
        ],
        compiler_params=pltpu.CompilerParams(vmem_limit_bytes=SMALL),
        cost_estimate=pl.CostEstimate(
            flops=4 * 10**8, bytes_accessed=5 * 10**6, transcendentals=0
        ),
        name="carry",
    )(w_mine, came)


def weight_kernel(
    c_ref, accmine_ref, wother_ref, came_ref, theirs_ref, dbc_ref, turned_hbm,
    gwmine_ref, gwother_ref, state_ref, turned_scr, sem,
):
    core = c_ref[0]
    is_first = core == 0
    starts = [pl.multiple_of(half * HALF_D, HALF_D) for half in (1 - core, core)]
    loads = [
        pltpu.make_async_copy(
            turned_hbm.at[pl.ds(start, HALF_D), :], turned_scr.at[n], sem.at[n]
        )
        for n, start in enumerate(starts)
    ]
    for load in loads:
        load.start()
    acc = jnp.zeros((T, N), F32)
    for q in range(G):
        for i in range(GT):
            rows = slice(8 * i, 8 * i + 8)
            lanes = slice(GL * q + 128 * i, GL * q + 128 * i + 128)
            tail = slice(STATE_ROWS + i, STATE_ROWS + i + 1)
            decay = theirs_ref[NM * q, tail, :]
            for m in range(0, NM, 2):
                at = NM * q + m
                pair = jnp.concatenate(
                    [
                        decay * came_ref[k, rows, :] + theirs_ref[k, rows, :]
                        for k in (at, at + 1)
                    ]
                )
                state_ref[8 * m : 8 * m + 16, lanes] = pair.astype(BF16)
        cols = slice(GL * q, GL * (q + 1))
        acc += mm_nt(wother_ref[:, cols], state_ref[:, cols])
    mine = accmine_ref[...]
    db = dbc_ref[:, :N] + jnp.where(is_first, acc, mine)
    dc = dbc_ref[:, N:] + jnp.where(is_first, mine, acc)
    dbc = (jnp.concatenate([db, dc], axis=1) * (1.0 / (T * 2 * CHIPS))).astype(BF16)
    for n, ref in enumerate((gwother_ref, gwmine_ref)):
        loads[n].wait()
        part = mm(turned_scr[n], dbc)
        ref[0] = part[:, :N]
        ref[1] = part[:, N:]


def weight_part(core, acc_mine, w_other, came, theirs, dbc, turned):
    return pl.pallas_call(
        weight_kernel,
        in_specs=[IN_SMEM] + [WHOLE] * 5 + [IN_HBM],
        out_specs=[WHOLE, WHOLE, WHOLE],
        out_shape=[
            jax.ShapeDtypeStruct((2, HALF_D, N), F32),
            jax.ShapeDtypeStruct((2, HALF_D, N), F32),
            jax.ShapeDtypeStruct((N, D), BF16),
        ],
        scratch_shapes=[
            pltpu.VMEM((2, HALF_D, T), BF16),
            pltpu.SemaphoreType.DMA((2,)),
        ],
        compiler_params=pltpu.CompilerParams(vmem_limit_bytes=MIDDLE),
        cost_estimate=pl.CostEstimate(
            flops=2 * 10**9, bytes_accessed=12 * 10**6, transcendentals=0
        ),
        name="weight_part",
    )(core, acc_mine, w_other, came, theirs, dbc, turned)


def outputs_kernel(
    c_ref, bc_ref, x_ref, dy_ref, cum_ref, cumt_ref, skip_ref, smine_ref, sother_ref, *refs,
):
    mixed_ref, gradx_ref, token_ref, scores, yacc, dxacc = refs[-6:]
    is_first = c_ref[0] == 0
    b_mat = bc_ref[:, :N]
    c_mat = bc_ref[:, N:]

    @pl.when(pl.program_id(0) == 0)
    def _():
        scores[...] = mm_nt(c_mat, b_mat)

    onehot = spread_matrix()
    cumt = cumt_ref[0]
    x = x_ref[...].astype(F32)
    dy = dy_ref[...].astype(F32)
    skip = skip_ref[...]
    mine = smine_ref[...].astype(F32)
    other = sother_ref[...].astype(F32)
    s_prev = jnp.where(is_first, mine, other).astype(BF16)
    g_next = jnp.where(is_first, other, mine).astype(BF16)
    fw = spread(jnp.exp(cumt), onehot)
    yacc[...] = skip * x + fw * mm(c_mat, s_prev)
    bw = spread(jnp.exp(cumt[T - 1 : T, :] - cumt), onehot)
    dxacc[...] = skip * dy + bw * mm(b_mat, g_next)
    for start, size in SPANS:
        lo, hi, u_lo, u_hi = span_weights(cumt, onehot, start, size)
        pair = scores[hi, lo].astype(BF16)
        yacc[hi, :] += u_hi * mm(pair, (x[lo, :] * u_lo).astype(BF16))
        dxacc[lo, :] += u_lo * mm_tn(pair, (dy[hi, :] * u_hi).astype(BF16))
    lower, first = chunk_masks()
    for chunk in range(T // CHUNK):
        rows = slice(chunk * CHUNK, (chunk + 1) * CHUNK)
        score = scores[rows, rows]
        for i in range(GT):
            lanes = slice(128 * i, 128 * i + 128)
            xt = x_ref[rows, lanes]
            dyt = dy_ref[rows, lanes]
            ys, dxs = [], []
            for e in range(2):
                decay = chunk_decay(cumt, cum_ref, rows, 2 * i + e, lower)
                mixing = (score * decay).astype(BF16)
                ys.append(mm(mixing, xt))
                dxs.append(mm_tn(mixing, dyt))
            mixed_ref[rows, lanes] = (
                yacc[rows, lanes] + jnp.where(first, ys[0], ys[1])
            ).astype(BF16)
            gradx_ref[rows, lanes] = (
                dxacc[rows, lanes] + jnp.where(first, dxs[0], dxs[1])
            ).astype(BF16)
    token_ref[0] = c_ref[0]


def outputs(core, bc, x, dy, cum, cumt, skip_row, s_mine, s_other, start, extra):
    cols = lambda rows=T: pl.BlockSpec((rows, GL), lambda q: (0, q + start))
    group = lambda *shape: pl.BlockSpec((1, *shape), lambda q: (q + start, 0, 0))
    return pl.pallas_call(
        outputs_kernel,
        grid=(G // 2,),
        in_specs=[
            IN_SMEM,
            full_spec(T, 2 * N),
            cols(),
            cols(),
            group(16, T),
            group(T, 128),
            cols(1),
            cols(N),
            cols(N),
        ]
        + [IN_HBM] * len(extra),
        out_specs=[cols(), cols(), IN_SMEM],
        out_shape=[
            jax.ShapeDtypeStruct((T, D), BF16),
            jax.ShapeDtypeStruct((T, D), BF16),
            TOKEN,
        ],
        scratch_shapes=[
            pltpu.VMEM((T, T), F32),
            pltpu.VMEM((T, GL), F32),
            pltpu.VMEM((T, GL), F32),
        ],
        input_output_aliases={9: 0, 10: 1} if len(extra) == 2 else {},
        compiler_params=pltpu.CompilerParams(vmem_limit_bytes=LARGE),
        cost_estimate=pl.CostEstimate(
            flops=12 * 10**9, bytes_accessed=7 * 10**6, transcendentals=2 * 10**6
        ),
        name="outputs",
    )(core, bc, x, dy, cum, cumt, skip_row, s_mine, s_other, *extra)


def add_kernel(a_ref, b_ref, out_hbm, scr, sem):
    block = HALF_D // 2
    stores = []
    for lane in range(2):
        for i in range(2):
            rows = pl.ds(block * i, block)
            scr[lane, rows, :] = a_ref[lane, rows, :] + b_ref[lane, rows, :]
            stores.append(
                pltpu.make_async_copy(
                    scr.at[lane, rows], out_hbm.at[lane, rows], sem.at[lane, i]
                )
            )
            stores[-1].start()
    for store in stores:
        store.wait()


def pair_add(a, b):
    return pl.pallas_call(
        add_kernel,
        in_specs=[WHOLE, WHOLE],
        out_specs=IN_HBM,
        out_shape=jax.ShapeDtypeStruct(a.shape, F32),
        scratch_shapes=[
            pltpu.VMEM(a.shape, F32),
            pltpu.SemaphoreType.DMA((2, 2)),
        ],
        compiler_params=pltpu.CompilerParams(vmem_limit_bytes=MIDDLE),
        name="pair_add",
    )(a, b)


def plane_kernel(in_ref, after_ref, out_ref):
    out_ref[...] = jnp.sum(in_ref[...], axis=0)


def plane_total(parts, after):
    return pl.pallas_call(
        plane_kernel,
        in_specs=[WHOLE, IN_SMEM],
        out_specs=WHOLE,
        out_shape=jax.ShapeDtypeStruct((GW_ROWS, 128), F32),
        compiler_params=pltpu.CompilerParams(vmem_limit_bytes=SMALL),
        name="plane_total",
    )(parts, after)


def chips_kernel(c_ref, z_ref, own_ref, back1_ref, back2_ref, back3_ref, out_ref, token_ref):
    z = z_ref[0]
    held = [own_ref[...], back1_ref[...], back2_ref[...], back3_ref[...]]
    total = None
    for plane in range(4):
        behind = jnp.bitwise_and(z - plane, 3)
        part = held[3]
        for k in range(3):
            part = jnp.where(behind == k, held[k], part)
        total = part if total is None else total + part
    for k in range(PLANE):
        out_ref[k] = total
    token_ref[0] = c_ref[0]


def chips_total(core, z, own):
    others = [
        lax.ppermute(own, "z", [(i, (i + k) % 4) for i in range(4)]) for k in (1, 2, 3)
    ]
    return pl.pallas_call(
        chips_kernel,
        in_specs=[IN_SMEM] * 2 + [WHOLE] * 4,
        out_specs=[WHOLE, IN_SMEM],
        out_shape=[jax.ShapeDtypeStruct((PLANE, GW_ROWS, 128), F32), TOKEN],
        compiler_params=pltpu.CompilerParams(vmem_limit_bytes=SMALL),
        name="chips_total",
    )(core, z, own, *others)


def hold_kernel(c_ref, in_ref, out_ref, token_ref):
    out_ref[...] = in_ref[...]
    token_ref[0] = c_ref[0]


def hold(core, half):
    return pl.pallas_call(
        hold_kernel,
        in_specs=[IN_SMEM, WHOLE],
        out_specs=[WHOLE, IN_SMEM],
        out_shape=[jax.ShapeDtypeStruct(half.shape, F32), TOKEN],
        compiler_params=pltpu.CompilerParams(vmem_limit_bytes=SMALL),
        name="hold",
    )(core, half)


def place_kernel(c_ref, half_ref, *refs):
    out_ref = refs[-1]
    for lane in range(2):
        out_ref[:, 128 * lane : 128 * lane + 128] = half_ref[lane]


def place(at, half, into):
    block = HALF_D // 2
    extra = [] if into is None else [into]
    return pl.pallas_call(
        place_kernel,
        grid_spec=pltpu.PrefetchScalarGridSpec(
            num_scalar_prefetch=1,
            grid=(2,),
            in_specs=[pl.BlockSpec((2, block, 128), lambda i, c: (0, i, 0))]
            + [pl.BlockSpec(memory_space=pl.ANY)] * len(extra),
            out_specs=pl.BlockSpec((block, 2 * N), lambda i, c: (2 * c[0] + i, 0)),
        ),
        out_shape=jax.ShapeDtypeStruct((D, 2 * N), F32),
        input_output_aliases={2: 0} if extra else {},
        compiler_params=pltpu.CompilerParams(vmem_limit_bytes=SMALL),
        name="place",
    )(at, half, *extra)


def swap(v):
    return lax.ppermute(v, "c", [(0, 1), (1, 0)])


def exchange(v, axes=CHIP_AXES):
    return lax.all_to_all(v, axes, 0, 0, tiled=True)


def shards(hidden, w_bc, ssm_in, codes, rates, skip, grad_out):
    core = lax.axis_index("c").astype(jnp.int32).reshape(1)
    skip_row = jnp.repeat(skip, PS)[None, :]
    bc, cum, cumt, mine, other = pre(
        core, hidden, w_bc, ssm_in, grad_out, codes, rates[None, :]
    )
    chip = chip_sum(mine, swap(other))
    slices = exchange(chip)
    theirs = swap(mine)
    w_mine, w_other, dbc, turned, paired = pairs(
        core, bc, ssm_in, grad_out, cum, cumt, hidden, chip
    )
    came = exchange(scan_chips(core, slices, paired))
    acc_mine, s_mine = carry(w_mine, came)
    gw_mine, gw_other, s_other = weight_part(
        core, acc_mine, w_other, swap(came), theirs, dbc, turned
    )
    part = pair_add(gw_mine, swap(gw_other))
    sums = exchange(part.reshape(PLANE, GW_ROWS, 128), ("x", "y"))
    pieces = (bc, ssm_in, grad_out, cum, cumt, skip_row, s_mine, s_other)
    mixed, gradx, done = outputs(core, *pieces, 0, [part])
    z = lax.axis_index("z").astype(jnp.int32).reshape(1)
    total, core_after = chips_total(core, z, plane_total(sums, done))
    half = exchange(total, ("x", "y")).reshape(2, HALF_D, 128)
    mixed, gradx, core_after = outputs(core_after, *pieces, G // 2, [mixed, gradx])
    half, core_after = hold(core_after, half)
    grad_w = place(1 - core, swap(half), place(core_after, half, None))
    return mixed, gradx, grad_w


def solution(mesh):
    grid = Mesh(mesh.devices.reshape(4, 4, 4, 2), ALL_AXES)
    rows = P(ALL_AXES, None)
    return jax.shard_map(
        shards,
        mesh=grid,
        in_specs=(rows, P(), rows, P(None, ALL_AXES), P(), P(), rows),
        out_specs=(rows, rows, P()),
        check_vma=False,
    )
```

```python
import functools

import jax
import jax.numpy as jnp
from jax import lax
from jax.experimental import pallas as pl
from jax.experimental.pallas import tpu as pltpu
from jax.sharding import Mesh
from jax.sharding import PartitionSpec as P

F32 = jnp.float32
BF16 = jnp.bfloat16
CHIP_AXES = ("z", "x", "y")
ALL_AXES = ("z", "x", "y", "c")
T = 512
H = 40
PS = 64
N = 128
D = 2560
G = 4
GH = H // G
GL = GH * PS
GT = GL // 128
NM = N // 8
CHIPS = 64
STATE_ROWS = 8 * GT
ROWS = 48
HALF_D = D // 2
GW_ROWS = 2 * HALF_D // CHIPS
KC = 5
KL = D // KC
LARGE = 56 << 20
MIDDLE = 44 << 20
SMALL = 10 << 20
WHOLE = pl.BlockSpec(memory_space=pltpu.VMEM)
IN_HBM = pl.BlockSpec(memory_space=pltpu.HBM)
IN_SMEM = pl.BlockSpec(memory_space=pltpu.SMEM)
TOKEN = jax.ShapeDtypeStruct((1,), jnp.int32)


def mm(a, b):
    return jnp.dot(a, b, preferred_element_type=F32)


def mm_nt(a, b):
    return lax.dot_general(a, b, (((1,), (1,)), ((), ())), preferred_element_type=F32)


def mm_tn(a, b):
    return lax.dot_general(a, b, (((0,), (0,)), ((), ())), preferred_element_type=F32)


def spread_matrix():
    k = lax.broadcasted_iota(jnp.int32, (128, GL), 0)
    col = lax.broadcasted_iota(jnp.int32, (128, GL), 1)
    return jnp.where((k & 63) == (col >> 6), 1.0, 0.0).astype(BF16)


def spread(v, onehot):
    high = v.astype(BF16).astype(F32)
    low = pltpu.roll(v - high, 64, 1)
    lane = lax.broadcasted_iota(jnp.int32, v.shape, 1)
    return mm(jnp.where(lane < 64, high, low).astype(BF16), onehot)


def pre_kernel(
    c_ref, rates_ref, hidden_hbm, w_hbm, x_hbm, dy_hbm, codes_hbm,
    bc_hbm, cum_hbm, cumt_hbm, mine_hbm, other_hbm,
    hidden_scr, w_scr, x_scr, dy_scr, codes_scr, bc_scr, cum_scr, cumt_scr, mine_scr, other_scr,
    in_sem, out_sem, small_sem,
):
    is_first = c_ref[0] == 0
    cols = [pl.ds(GL * q, GL) for q in range(G)]
    code_load = pltpu.make_async_copy(codes_hbm, codes_scr, small_sem.at[0])
    code_load.start()
    loads = {}
    for n, (src, dst) in enumerate(((x_hbm, x_scr), (dy_hbm, dy_scr))):
        for q in range(G):
            loads[n, q] = pltpu.make_async_copy(
                src.at[:, cols[q]], dst.at[q], in_sem.at[n, q]
            )
    for q in range(KC):
        part = pl.ds(KL * q, KL)
        loads[2, q] = pltpu.make_async_copy(
            hidden_hbm.at[:, part], hidden_scr.at[q], in_sem.at[2, q]
        )
        loads[3, q] = pltpu.make_async_copy(
            w_hbm.at[part, :], w_scr.at[q], in_sem.at[3, q]
        )
    waves = [(loads[2, q], loads[3, q]) for q in range(KC)]
    waves += [(loads[0, q], loads[1, q]) for q in range(G)]
    ahead = 5

    def take(n):
        for load in waves[n]:
            load.wait()
        if n + ahead < len(waves):
            for load in waves[n + ahead]:
                load.start()

    for wave in waves[:ahead]:
        for load in wave:
            load.start()

    eye = lax.broadcasted_iota(jnp.int32, (H, H), 0) == lax.broadcasted_iota(
        jnp.int32, (H, H), 1
    )
    rates = jnp.sum(jnp.where(eye, rates_ref[...], 0.0), axis=1, keepdims=True)
    s_at = lax.broadcasted_iota(jnp.int32, (T, T), 0)
    t_at = lax.broadcasted_iota(jnp.int32, (T, T), 1)
    upper = jnp.where(s_at <= t_at, 1.0, 0.0).astype(BF16)
    onehot = spread_matrix()
    cum_scr[...] = jnp.zeros_like(cum_scr)
    code_load.wait()
    code = codes_scr[...].astype(F32)
    step = -(
        rates * jnp.minimum(code, 1000.0) / 1000.0
        + 0.0005 * jnp.maximum(code - 1000.0, 0.0)
    )
    p1 = step.astype(BF16)
    rest = step - p1.astype(F32)
    p2 = rest.astype(BF16)
    p3 = (rest - p2.astype(F32)).astype(BF16)
    sums = mm(jnp.concatenate([p1, p2, p3, jnp.zeros((8, T), BF16)]), upper)
    cum = sums[0:H] + sums[H : 2 * H] + sums[2 * H : 3 * H]
    by_token = jnp.concatenate([cum, jnp.zeros((128 - H, T), F32)]).T
    stores = []

    def send(src, dst, sem):
        stores.append(pltpu.make_async_copy(src, dst, sem))
        stores[-1].start()

    for q in range(G):
        cum_scr[q, 0:GH, :] = cum[GH * q : GH * (q + 1), :]
        cumt_scr[q] = by_token if q == 0 else pltpu.roll(by_token, 128 - GH * q, 1)
    send(cum_scr, cum_hbm, small_sem.at[1])
    send(cumt_scr, cumt_hbm, small_sem.at[2])
    for q in range(KC):
        take(q)
    depth = [hidden_scr[q] for q in range(KC)]
    acc = mm(jnp.concatenate(depth, axis=1), w_scr[...].reshape(D, 2 * N))
    bc_scr[...] = acc.astype(BF16)
    send(bc_scr, bc_hbm, small_sem.at[3])
    bt = bc_scr[:, :N].T
    ct = bc_scr[:, N:].T
    for q in range(G):
        cumt = cumt_scr[q]
        total = cumt[T - 1 : T, :]
        fw = spread(jnp.exp(cumt), onehot)
        decay = fw[T - 1 : T, :]
        bw = spread(jnp.exp(total - cumt), onehot)
        take(KC + q)
        sf = mm(bt, (x_scr[q].astype(F32) * bw).astype(BF16))
        sb = mm(ct, (dy_scr[q].astype(F32) * fw).astype(BF16))
        rows = pl.ds(NM * q, NM)
        for n, (scr, hbm, state) in enumerate(
            (
                (other_scr, other_hbm, jnp.where(is_first, sb, sf)),
                (mine_scr, mine_hbm, jnp.where(is_first, sf, sb)),
            )
        ):
            for m in range(NM):
                for i in range(GT):
                    lanes = slice(128 * i, 128 * i + 128)
                    scr[NM * q + m, 8 * i : 8 * i + 8, :] = state[8 * m : 8 * m + 8, lanes]
                    row = STATE_ROWS + i
                    scr[NM * q + m, row : row + 1, :] = decay[:, lanes]
                scr[NM * q + m, STATE_ROWS + GT : ROWS, :] = jnp.zeros(
                    (ROWS - STATE_ROWS - GT, 128), F32
                )
            send(scr.at[rows], hbm.at[rows], out_sem.at[n, q])
    for store in stores:
        store.wait()


def pre(core, hidden, w_bc, x, dy, codes, rates):
    return pl.pallas_call(
        pre_kernel,
        in_specs=[pl.BlockSpec(memory_space=pltpu.SMEM), WHOLE] + [IN_HBM] * 5,
        out_specs=[IN_HBM] * 5,
        out_shape=[
            jax.ShapeDtypeStruct((T, 2 * N), BF16),
            jax.ShapeDtypeStruct((G, 16, T), F32),
            jax.ShapeDtypeStruct((G, T, 128), F32),
            jax.ShapeDtypeStruct((CHIPS, ROWS, 128), F32),
            jax.ShapeDtypeStruct((CHIPS, ROWS, 128), F32),
        ],
        scratch_shapes=[
            pltpu.VMEM((KC, T, KL), BF16),
            pltpu.VMEM((KC, KL, 2 * N), BF16),
            pltpu.VMEM((G, T, GL), BF16),
            pltpu.VMEM((G, T, GL), BF16),
            pltpu.VMEM((H, T), jnp.int32),
            pltpu.VMEM((T, 2 * N), BF16),
            pltpu.VMEM((G, 16, T), F32),
            pltpu.VMEM((G, T, 128), F32),
            pltpu.VMEM((CHIPS, ROWS, 128), F32),
            pltpu.VMEM((CHIPS, ROWS, 128), F32),
            pltpu.SemaphoreType.DMA((4, KC)),
            pltpu.SemaphoreType.DMA((2, G)),
            pltpu.SemaphoreType.DMA((4,)),
        ],
        compiler_params=pltpu.CompilerParams(vmem_limit_bytes=LARGE),
        cost_estimate=pl.CostEstimate(
            flops=2 * 10**9, bytes_accessed=13 * 10**6, transcendentals=0
        ),
        name="pre",
    )(core, rates, hidden, w_bc, x, dy, codes)


def chip_kernel(mine_ref, got_ref, out_ref):
    for m in range(CHIPS):
        for i in range(GT):
            other = got_ref[m, STATE_ROWS + i : STATE_ROWS + i + 1, :]
            rows = slice(8 * i, 8 * i + 8)
            out_ref[m, rows, :] = other * mine_ref[m, rows, :] + got_ref[m, rows, :]
        tail = slice(STATE_ROWS, ROWS)
        out_ref[m, tail, :] = mine_ref[m, tail, :] * got_ref[m, tail, :]


def chip_sum(mine, got):
    return pl.pallas_call(
        chip_kernel,
        in_specs=[WHOLE, WHOLE],
        out_specs=WHOLE,
        out_shape=jax.ShapeDtypeStruct((CHIPS, ROWS, 128), F32),
        compiler_params=pltpu.CompilerParams(vmem_limit_bytes=SMALL),
        name="chip_sum",
    )(mine, got)


def scan_kernel(c_ref, in_ref, after_ref, out_ref):
    core = c_ref[0]
    state = [jnp.zeros((8, 128), F32) for _ in range(GT)]
    for k in range(CHIPS):
        at = k + core * (CHIPS - 1 - 2 * k)
        for i in range(GT):
            rows = slice(8 * i, 8 * i + 8)
            out_ref[at, rows, :] = state[i]
            decay = in_ref[at, STATE_ROWS + i : STATE_ROWS + i + 1, :]
            state[i] = decay * state[i] + in_ref[at, rows, :]


def scan_chips(core, slices, after):
    return pl.pallas_call(
        scan_kernel,
        in_specs=[IN_SMEM, WHOLE, IN_SMEM],
        out_specs=WHOLE,
        out_shape=jax.ShapeDtypeStruct((CHIPS, STATE_ROWS, 128), F32),
        compiler_params=pltpu.CompilerParams(vmem_limit_bytes=SMALL),
        name="scan_chips",
    )(core, slices, after)


SPANS = ((0, 256), (0, 128), (256, 128))
CHUNK = 128


def span_weights(cumt, onehot, start, size):
    lo = slice(start, start + size)
    hi = slice(start + size, start + 2 * size)
    edge = cumt[start + size - 1 : start + size, :]
    u_lo = spread(jnp.exp(edge - cumt[lo, :]), onehot)
    u_hi = spread(jnp.exp(cumt[hi, :] - edge), onehot)
    return lo, hi, u_lo, u_hi


def chunk_masks():
    t_at = lax.broadcasted_iota(jnp.int32, (CHUNK, CHUNK), 0)
    s_at = lax.broadcasted_iota(jnp.int32, (CHUNK, CHUNK), 1)
    return t_at >= s_at, s_at < PS


def chunk_decay(cumt, cum_ref, rows, h, lower):
    gap = cumt[rows, h : h + 1] - cum_ref[0, h : h + 1, rows]
    return jnp.exp(jnp.where(lower, gap, -jnp.inf))


def pairs_kernel(
    c_ref, bc_ref, x_ref, dy_ref, cum_ref, cumt_ref, hidden_ref, after_ref,
    wmine_ref, wother_ref, dbc_ref, turned_ref, token_ref, kmat,
):
    q = pl.program_id(0)
    is_first = c_ref[0] == 0

    @pl.when(q == 0)
    def _():
        kmat[...] = jnp.zeros_like(kmat)

    turned_ref[...] = hidden_ref[...].T
    onehot = spread_matrix()
    cumt = cumt_ref[0]
    x = x_ref[...].astype(F32)
    dy = dy_ref[...].astype(F32)
    wg = dy * spread(jnp.exp(cumt), onehot)
    wi = x * spread(jnp.exp(cumt[T - 1 : T, :] - cumt), onehot)
    wmine_ref[...] = jnp.where(is_first, wg, wi).astype(BF16)
    wother_ref[...] = jnp.where(is_first, wi, wg).astype(BF16)
    for start, size in SPANS:
        lo, hi, u_lo, u_hi = span_weights(cumt, onehot, start, size)
        kmat[hi, lo] += mm_nt((dy[hi, :] * u_hi).astype(BF16), (x[lo, :] * u_lo).astype(BF16))
    lower, first = chunk_masks()
    for chunk in range(T // CHUNK):
        rows = slice(chunk * CHUNK, (chunk + 1) * CHUNK)
        ksum = jnp.zeros((CHUNK, CHUNK), F32)
        for i in range(GT):
            lanes = slice(128 * i, 128 * i + 128)
            xt = x_ref[rows, lanes]
            dyf = dy[rows, lanes]
            for e in range(2):
                own = first if e == 0 else jnp.logical_not(first)
                dyh = jnp.where(own, dyf, 0.0).astype(BF16)
                ksum += chunk_decay(cumt, cum_ref, rows, 2 * i + e, lower) * mm_nt(dyh, xt)
        kmat[rows, rows] += ksum

    @pl.when(q == G - 1)
    def _():
        k = kmat[...].astype(BF16)
        dbc_ref[:, :N] = mm_tn(k, bc_ref[:, N:])
        dbc_ref[:, N:] = mm(k, bc_ref[:, :N])
        token_ref[0] = 0


def full_spec(*shape):
    return pl.BlockSpec(shape, lambda q: (0,) * len(shape))


def cols_spec(rows=T):
    return pl.BlockSpec((rows, GL), lambda q: (0, q))


def group_spec(*shape):
    return pl.BlockSpec((1, *shape), lambda q: (q, 0, 0))


def pairs(core, bc, x, dy, cum, cumt, hidden, after):
    return pl.pallas_call(
        pairs_kernel,
        grid=(G,),
        in_specs=[
            pl.BlockSpec(memory_space=pltpu.SMEM),
            full_spec(T, 2 * N),
            cols_spec(),
            cols_spec(),
            group_spec(16, T),
            group_spec(T, 128),
            cols_spec(),
            IN_HBM,
        ],
        out_specs=[
            cols_spec(),
            cols_spec(),
            full_spec(T, 2 * N),
            pl.BlockSpec((GL, T), lambda q: (q, 0)),
            IN_SMEM,
        ],
        out_shape=[
            jax.ShapeDtypeStruct((T, D), BF16),
            jax.ShapeDtypeStruct((T, D), BF16),
            jax.ShapeDtypeStruct((T, 2 * N), F32),
            jax.ShapeDtypeStruct((D, T), BF16),
            TOKEN,
        ],
        scratch_shapes=[pltpu.VMEM((T, T), F32)],
        compiler_params=pltpu.CompilerParams(vmem_limit_bytes=LARGE),
        cost_estimate=pl.CostEstimate(
            flops=20 * 10**9, bytes_accessed=16 * 10**6, transcendentals=3 * 10**6
        ),
        name="pairs",
    )(core, bc, x, dy, cum, cumt, hidden, after)


def carry_kernel(w_ref, came_ref, acc_ref, state_ref):
    acc = jnp.zeros((T, N), F32)
    for q in range(G):
        for i in range(GT):
            rows = slice(8 * i, 8 * i + 8)
            lanes = slice(GL * q + 128 * i, GL * q + 128 * i + 128)
            for m in range(0, NM, 2):
                at = NM * q + m
                pair = jnp.concatenate([came_ref[at, rows, :], came_ref[at + 1, rows, :]])
                state_ref[8 * m : 8 * m + 16, lanes] = pair.astype(BF16)
        cols = slice(GL * q, GL * (q + 1))
        acc += mm_nt(w_ref[:, cols], state_ref[:, cols])
    acc_ref[...] = acc


def carry(w_mine, came):
    return pl.pallas_call(
        carry_kernel,
        in_specs=[WHOLE, WHOLE],
        out_specs=[WHOLE, WHOLE],
        out_shape=[
            jax.ShapeDtypeStruct((T, N), F32),
            jax.ShapeDtypeStruct((N, D), BF16),
        ],
        compiler_params=pltpu.CompilerParams(vmem_limit_bytes=SMALL),
        cost_estimate=pl.CostEstimate(
            flops=4 * 10**8, bytes_accessed=5 * 10**6, transcendentals=0
        ),
        name="carry",
    )(w_mine, came)


def weight_kernel(
    c_ref, accmine_ref, wother_ref, came_ref, theirs_ref, dbc_ref, turned_hbm,
    gwmine_ref, gwother_ref, state_ref, turned_scr, sem,
):
    core = c_ref[0]
    is_first = core == 0
    starts = [pl.multiple_of(half * HALF_D, HALF_D) for half in (1 - core, core)]
    loads = [
        pltpu.make_async_copy(
            turned_hbm.at[pl.ds(start, HALF_D), :], turned_scr.at[n], sem.at[n]
        )
        for n, start in enumerate(starts)
    ]
    for load in loads:
        load.start()
    acc = jnp.zeros((T, N), F32)
    for q in range(G):
        for i in range(GT):
            rows = slice(8 * i, 8 * i + 8)
            lanes = slice(GL * q + 128 * i, GL * q + 128 * i + 128)
            tail = slice(STATE_ROWS + i, STATE_ROWS + i + 1)
            decay = theirs_ref[NM * q, tail, :]
            for m in range(0, NM, 2):
                at = NM * q + m
                pair = jnp.concatenate(
                    [
                        decay * came_ref[k, rows, :] + theirs_ref[k, rows, :]
                        for k in (at, at + 1)
                    ]
                )
                state_ref[8 * m : 8 * m + 16, lanes] = pair.astype(BF16)
        cols = slice(GL * q, GL * (q + 1))
        acc += mm_nt(wother_ref[:, cols], state_ref[:, cols])
    mine = accmine_ref[...]
    db = dbc_ref[:, :N] + jnp.where(is_first, acc, mine)
    dc = dbc_ref[:, N:] + jnp.where(is_first, mine, acc)
    dbc = (jnp.concatenate([db, dc], axis=1) * (1.0 / (T * 2 * CHIPS))).astype(BF16)
    for n, ref in enumerate((gwother_ref, gwmine_ref)):
        loads[n].wait()
        part = mm(turned_scr[n], dbc)
        ref[0] = part[:, :N]
        ref[1] = part[:, N:]


def weight_part(core, acc_mine, w_other, came, theirs, dbc, turned):
    return pl.pallas_call(
        weight_kernel,
        in_specs=[IN_SMEM] + [WHOLE] * 5 + [IN_HBM],
        out_specs=[WHOLE, WHOLE, WHOLE],
        out_shape=[
            jax.ShapeDtypeStruct((2, HALF_D, N), F32),
            jax.ShapeDtypeStruct((2, HALF_D, N), F32),
            jax.ShapeDtypeStruct((N, D), BF16),
        ],
        scratch_shapes=[
            pltpu.VMEM((2, HALF_D, T), BF16),
            pltpu.SemaphoreType.DMA((2,)),
        ],
        compiler_params=pltpu.CompilerParams(vmem_limit_bytes=MIDDLE),
        cost_estimate=pl.CostEstimate(
            flops=2 * 10**9, bytes_accessed=12 * 10**6, transcendentals=0
        ),
        name="weight_part",
    )(core, acc_mine, w_other, came, theirs, dbc, turned)


def outputs_kernel(
    c_ref, bc_ref, x_ref, dy_ref, cum_ref, cumt_ref, skip_ref, smine_ref, sother_ref, *refs,
):
    mixed_ref, gradx_ref, token_ref, scores, yacc, dxacc = refs[-6:]
    is_first = c_ref[0] == 0
    b_mat = bc_ref[:, :N]
    c_mat = bc_ref[:, N:]

    @pl.when(pl.program_id(0) == 0)
    def _():
        scores[...] = mm_nt(c_mat, b_mat)

    onehot = spread_matrix()
    cumt = cumt_ref[0]
    x = x_ref[...].astype(F32)
    dy = dy_ref[...].astype(F32)
    skip = skip_ref[...]
    mine = smine_ref[...].astype(F32)
    other = sother_ref[...].astype(F32)
    s_prev = jnp.where(is_first, mine, other).astype(BF16)
    g_next = jnp.where(is_first, other, mine).astype(BF16)
    fw = spread(jnp.exp(cumt), onehot)
    yacc[...] = skip * x + fw * mm(c_mat, s_prev)
    bw = spread(jnp.exp(cumt[T - 1 : T, :] - cumt), onehot)
    dxacc[...] = skip * dy + bw * mm(b_mat, g_next)
    for start, size in SPANS:
        lo, hi, u_lo, u_hi = span_weights(cumt, onehot, start, size)
        pair = scores[hi, lo].astype(BF16)
        yacc[hi, :] += u_hi * mm(pair, (x[lo, :] * u_lo).astype(BF16))
        dxacc[lo, :] += u_lo * mm_tn(pair, (dy[hi, :] * u_hi).astype(BF16))
    lower, first = chunk_masks()
    for chunk in range(T // CHUNK):
        rows = slice(chunk * CHUNK, (chunk + 1) * CHUNK)
        score = scores[rows, rows]
        for i in range(GT):
            lanes = slice(128 * i, 128 * i + 128)
            xt = x_ref[rows, lanes]
            dyt = dy_ref[rows, lanes]
            ys, dxs = [], []
            for e in range(2):
                decay = chunk_decay(cumt, cum_ref, rows, 2 * i + e, lower)
                mixing = (score * decay).astype(BF16)
                ys.append(mm(mixing, xt))
                dxs.append(mm_tn(mixing, dyt))
            mixed_ref[rows, lanes] = (
                yacc[rows, lanes] + jnp.where(first, ys[0], ys[1])
            ).astype(BF16)
            gradx_ref[rows, lanes] = (
                dxacc[rows, lanes] + jnp.where(first, dxs[0], dxs[1])
            ).astype(BF16)
    token_ref[0] = c_ref[0]


def outputs(core, bc, x, dy, cum, cumt, skip_row, s_mine, s_other, start, extra):
    cols = lambda rows=T: pl.BlockSpec((rows, GL), lambda q: (0, q + start))
    group = lambda *shape: pl.BlockSpec((1, *shape), lambda q: (q + start, 0, 0))
    return pl.pallas_call(
        outputs_kernel,
        grid=(G // 2,),
        in_specs=[
            IN_SMEM,
            full_spec(T, 2 * N),
            cols(),
            cols(),
            group(16, T),
            group(T, 128),
            cols(1),
            cols(N),
            cols(N),
        ]
        + [IN_HBM] * len(extra),
        out_specs=[cols(), cols(), IN_SMEM],
        out_shape=[
            jax.ShapeDtypeStruct((T, D), BF16),
            jax.ShapeDtypeStruct((T, D), BF16),
            TOKEN,
        ],
        scratch_shapes=[
            pltpu.VMEM((T, T), F32),
            pltpu.VMEM((T, GL), F32),
            pltpu.VMEM((T, GL), F32),
        ],
        input_output_aliases={9: 0, 10: 1} if len(extra) == 2 else {},
        compiler_params=pltpu.CompilerParams(vmem_limit_bytes=LARGE),
        cost_estimate=pl.CostEstimate(
            flops=12 * 10**9, bytes_accessed=7 * 10**6, transcendentals=2 * 10**6
        ),
        name="outputs",
    )(core, bc, x, dy, cum, cumt, skip_row, s_mine, s_other, *extra)


def add_kernel(a_ref, b_ref, out_hbm, scr, sem):
    block = HALF_D // 2
    stores = []
    for lane in range(2):
        for i in range(2):
            rows = pl.ds(block * i, block)
            scr[lane, rows, :] = a_ref[lane, rows, :] + b_ref[lane, rows, :]
            stores.append(
                pltpu.make_async_copy(
                    scr.at[lane, rows], out_hbm.at[lane, rows], sem.at[lane, i]
                )
            )
            stores[-1].start()
    for store in stores:
        store.wait()


def pair_add(a, b):
    return pl.pallas_call(
        add_kernel,
        in_specs=[WHOLE, WHOLE],
        out_specs=IN_HBM,
        out_shape=jax.ShapeDtypeStruct(a.shape, F32),
        scratch_shapes=[
            pltpu.VMEM(a.shape, F32),
            pltpu.SemaphoreType.DMA((2, 2)),
        ],
        compiler_params=pltpu.CompilerParams(vmem_limit_bytes=MIDDLE),
        name="pair_add",
    )(a, b)


def total_kernel(c_ref, in_ref, out_ref, token_ref):
    total = jnp.sum(in_ref[...], axis=0)
    for k in range(CHIPS):
        out_ref[k] = total
    token_ref[0] = c_ref[0]


def chip_total(core, parts):
    return pl.pallas_call(
        total_kernel,
        in_specs=[IN_SMEM, WHOLE],
        out_specs=[WHOLE, IN_SMEM],
        out_shape=[jax.ShapeDtypeStruct((CHIPS, GW_ROWS, 128), F32), TOKEN],
        compiler_params=pltpu.CompilerParams(vmem_limit_bytes=SMALL),
        name="chip_total",
    )(core, parts)


def hold_kernel(c_ref, in_ref, out_ref, token_ref):
    out_ref[...] = in_ref[...]
    token_ref[0] = c_ref[0]


def hold(core, half):
    return pl.pallas_call(
        hold_kernel,
        in_specs=[IN_SMEM, WHOLE],
        out_specs=[WHOLE, IN_SMEM],
        out_shape=[jax.ShapeDtypeStruct(half.shape, F32), TOKEN],
        compiler_params=pltpu.CompilerParams(vmem_limit_bytes=SMALL),
        name="hold",
    )(core, half)


def place_kernel(c_ref, half_ref, *refs):
    out_ref = refs[-1]
    for lane in range(2):
        out_ref[:, 128 * lane : 128 * lane + 128] = half_ref[lane]


def place(at, half, into):
    block = HALF_D // 2
    extra = [] if into is None else [into]
    return pl.pallas_call(
        place_kernel,
        grid_spec=pltpu.PrefetchScalarGridSpec(
            num_scalar_prefetch=1,
            grid=(2,),
            in_specs=[pl.BlockSpec((2, block, 128), lambda i, c: (0, i, 0))]
            + [pl.BlockSpec(memory_space=pl.ANY)] * len(extra),
            out_specs=pl.BlockSpec((block, 2 * N), lambda i, c: (2 * c[0] + i, 0)),
        ),
        out_shape=jax.ShapeDtypeStruct((D, 2 * N), F32),
        input_output_aliases={2: 0} if extra else {},
        compiler_params=pltpu.CompilerParams(vmem_limit_bytes=SMALL),
        name="place",
    )(at, half, *extra)


def swap(v):
    return lax.ppermute(v, "c", [(0, 1), (1, 0)])


def exchange(v):
    return lax.all_to_all(v, CHIP_AXES, 0, 0, tiled=True)


def shards(hidden, w_bc, ssm_in, codes, rates, skip, grad_out):
    core = lax.axis_index("c").astype(jnp.int32).reshape(1)
    skip_row = jnp.repeat(skip, PS)[None, :]
    bc, cum, cumt, mine, other = pre(
        core, hidden, w_bc, ssm_in, grad_out, codes, rates[None, :]
    )
    chip = chip_sum(mine, swap(other))
    slices = exchange(chip)
    theirs = swap(mine)
    w_mine, w_other, dbc, turned, paired = pairs(
        core, bc, ssm_in, grad_out, cum, cumt, hidden, chip
    )
    came = exchange(scan_chips(core, slices, paired))
    acc_mine, s_mine = carry(w_mine, came)
    gw_mine, gw_other, s_other = weight_part(
        core, acc_mine, w_other, swap(came), theirs, dbc, turned
    )
    part = pair_add(gw_mine, swap(gw_other))
    sums = exchange(part.reshape(CHIPS, GW_ROWS, 128))
    pieces = (bc, ssm_in, grad_out, cum, cumt, skip_row, s_mine, s_other)
    mixed, gradx, core_after = outputs(core, *pieces, 0, [part])
    total, core_after = chip_total(core_after, sums)
    half = exchange(total).reshape(2, HALF_D, 128)
    mixed, gradx, core_after = outputs(core_after, *pieces, G // 2, [mixed, gradx])
    half, core_after = hold(core_after, half)
    grad_w = place(1 - core, swap(half), place(core_after, half, None))
    return mixed, gradx, grad_w


def solution(mesh):
    grid = Mesh(mesh.devices.reshape(4, 4, 4, 2), ALL_AXES)
    rows = P(ALL_AXES, None)
    return jax.shard_map(
        shards,
        mesh=grid,
        in_specs=(rows, P(), rows, P(None, ALL_AXES), P(), P(), rows),
        out_specs=(rows, rows, P()),
        check_vma=False,
    )
```

```python
import functools

import jax
import jax.numpy as jnp
from jax import lax
from jax.experimental import pallas as pl
from jax.experimental.pallas import tpu as pltpu
from jax.sharding import Mesh
from jax.sharding import PartitionSpec as P

F32 = jnp.float32
BF16 = jnp.bfloat16
CHIP_AXES = ("z", "x", "y")
ALL_AXES = ("z", "x", "y", "c")
T = 512
H = 40
PS = 64
N = 128
D = 2560
G = 4
GH = H // G
GL = GH * PS
GT = GL // 128
NM = N // 8
CHIPS = 64
STATE_ROWS = 8 * GT
ROWS = 48
HALF_D = D // 2
GW_ROWS = 2 * HALF_D // CHIPS
KC = 5
KL = D // KC
LARGE = 56 << 20
MIDDLE = 44 << 20
SMALL = 10 << 20
WHOLE = pl.BlockSpec(memory_space=pltpu.VMEM)
IN_HBM = pl.BlockSpec(memory_space=pltpu.HBM)
IN_SMEM = pl.BlockSpec(memory_space=pltpu.SMEM)
TOKEN = jax.ShapeDtypeStruct((1,), jnp.int32)


def mm(a, b):
    return jnp.dot(a, b, preferred_element_type=F32)


def mm_nt(a, b):
    return lax.dot_general(a, b, (((1,), (1,)), ((), ())), preferred_element_type=F32)


def mm_tn(a, b):
    return lax.dot_general(a, b, (((0,), (0,)), ((), ())), preferred_element_type=F32)


def spread_matrix():
    k = lax.broadcasted_iota(jnp.int32, (128, GL), 0)
    col = lax.broadcasted_iota(jnp.int32, (128, GL), 1)
    return jnp.where((k & 63) == (col >> 6), 1.0, 0.0).astype(BF16)


def spread(v, onehot):
    high = v.astype(BF16).astype(F32)
    low = pltpu.roll(v - high, 64, 1)
    lane = lax.broadcasted_iota(jnp.int32, v.shape, 1)
    return mm(jnp.where(lane < 64, high, low).astype(BF16), onehot)


def pre_kernel(
    c_ref, rates_ref, hidden_hbm, w_hbm, x_hbm, dy_hbm, codes_hbm,
    bc_hbm, cum_hbm, cumt_hbm, mine_hbm, other_hbm,
    hidden_scr, w_scr, x_scr, dy_scr, codes_scr, bc_scr, cum_scr, cumt_scr, mine_scr, other_scr,
    in_sem, out_sem, small_sem,
):
    is_first = c_ref[0] == 0
    cols = [pl.ds(GL * q, GL) for q in range(G)]
    code_load = pltpu.make_async_copy(codes_hbm, codes_scr, small_sem.at[0])
    code_load.start()
    loads = {}
    for n, (src, dst) in enumerate(((x_hbm, x_scr), (dy_hbm, dy_scr))):
        for q in range(G):
            loads[n, q] = pltpu.make_async_copy(
                src.at[:, cols[q]], dst.at[q], in_sem.at[n, q]
            )
    for q in range(KC):
        part = pl.ds(KL * q, KL)
        loads[2, q] = pltpu.make_async_copy(
            hidden_hbm.at[:, part], hidden_scr.at[q], in_sem.at[2, q]
        )
        loads[3, q] = pltpu.make_async_copy(
            w_hbm.at[part, :], w_scr.at[q], in_sem.at[3, q]
        )
    waves = [(loads[2, q], loads[3, q]) for q in range(KC)]
    waves += [(loads[0, q], loads[1, q]) for q in range(G)]
    ahead = 5

    def take(n):
        for load in waves[n]:
            load.wait()
        if n + ahead < len(waves):
            for load in waves[n + ahead]:
                load.start()

    for wave in waves[:ahead]:
        for load in wave:
            load.start()

    eye = lax.broadcasted_iota(jnp.int32, (H, H), 0) == lax.broadcasted_iota(
        jnp.int32, (H, H), 1
    )
    rates = jnp.sum(jnp.where(eye, rates_ref[...], 0.0), axis=1, keepdims=True)
    s_at = lax.broadcasted_iota(jnp.int32, (T, T), 0)
    t_at = lax.broadcasted_iota(jnp.int32, (T, T), 1)
    upper = jnp.where(s_at <= t_at, 1.0, 0.0).astype(BF16)
    onehot = spread_matrix()
    cum_scr[...] = jnp.zeros_like(cum_scr)
    code_load.wait()
    code = codes_scr[...].astype(F32)
    step = -(
        rates * jnp.minimum(code, 1000.0) / 1000.0
        + 0.0005 * jnp.maximum(code - 1000.0, 0.0)
    )
    p1 = step.astype(BF16)
    rest = step - p1.astype(F32)
    p2 = rest.astype(BF16)
    p3 = (rest - p2.astype(F32)).astype(BF16)
    sums = mm(jnp.concatenate([p1, p2, p3, jnp.zeros((8, T), BF16)]), upper)
    cum = sums[0:H] + sums[H : 2 * H] + sums[2 * H : 3 * H]
    by_token = jnp.concatenate([cum, jnp.zeros((128 - H, T), F32)]).T
    stores = []

    def send(src, dst, sem):
        stores.append(pltpu.make_async_copy(src, dst, sem))
        stores[-1].start()

    for q in range(G):
        cum_scr[q, 0:GH, :] = cum[GH * q : GH * (q + 1), :]
        cumt_scr[q] = by_token if q == 0 else pltpu.roll(by_token, 128 - GH * q, 1)
    send(cum_scr, cum_hbm, small_sem.at[1])
    send(cumt_scr, cumt_hbm, small_sem.at[2])
    for q in range(KC):
        take(q)
    depth = [hidden_scr[q] for q in range(KC)]
    acc = mm(jnp.concatenate(depth, axis=1), w_scr[...].reshape(D, 2 * N))
    bc_scr[...] = acc.astype(BF16)
    send(bc_scr, bc_hbm, small_sem.at[3])
    bt = bc_scr[:, :N].T
    ct = bc_scr[:, N:].T
    for q in range(G):
        cumt = cumt_scr[q]
        total = cumt[T - 1 : T, :]
        fw = spread(jnp.exp(cumt), onehot)
        decay = fw[T - 1 : T, :]
        bw = spread(jnp.exp(total - cumt), onehot)
        take(KC + q)
        sf = mm(bt, (x_scr[q].astype(F32) * bw).astype(BF16))
        sb = mm(ct, (dy_scr[q].astype(F32) * fw).astype(BF16))
        rows = pl.ds(NM * q, NM)
        for n, (scr, hbm, state) in enumerate(
            (
                (other_scr, other_hbm, jnp.where(is_first, sb, sf)),
                (mine_scr, mine_hbm, jnp.where(is_first, sf, sb)),
            )
        ):
            for m in range(NM):
                for i in range(GT):
                    lanes = slice(128 * i, 128 * i + 128)
                    scr[NM * q + m, 8 * i : 8 * i + 8, :] = state[8 * m : 8 * m + 8, lanes]
                    row = STATE_ROWS + i
                    scr[NM * q + m, row : row + 1, :] = decay[:, lanes]
                scr[NM * q + m, STATE_ROWS + GT : ROWS, :] = jnp.zeros(
                    (ROWS - STATE_ROWS - GT, 128), F32
                )
            send(scr.at[rows], hbm.at[rows], out_sem.at[n, q])
    for store in stores:
        store.wait()


def pre(core, hidden, w_bc, x, dy, codes, rates):
    return pl.pallas_call(
        pre_kernel,
        in_specs=[pl.BlockSpec(memory_space=pltpu.SMEM), WHOLE] + [IN_HBM] * 5,
        out_specs=[IN_HBM] * 5,
        out_shape=[
            jax.ShapeDtypeStruct((T, 2 * N), BF16),
            jax.ShapeDtypeStruct((G, 16, T), F32),
            jax.ShapeDtypeStruct((G, T, 128), F32),
            jax.ShapeDtypeStruct((CHIPS, ROWS, 128), F32),
            jax.ShapeDtypeStruct((CHIPS, ROWS, 128), F32),
        ],
        scratch_shapes=[
            pltpu.VMEM((KC, T, KL), BF16),
            pltpu.VMEM((KC, KL, 2 * N), BF16),
            pltpu.VMEM((G, T, GL), BF16),
            pltpu.VMEM((G, T, GL), BF16),
            pltpu.VMEM((H, T), jnp.int32),
            pltpu.VMEM((T, 2 * N), BF16),
            pltpu.VMEM((G, 16, T), F32),
            pltpu.VMEM((G, T, 128), F32),
            pltpu.VMEM((CHIPS, ROWS, 128), F32),
            pltpu.VMEM((CHIPS, ROWS, 128), F32),
            pltpu.SemaphoreType.DMA((4, KC)),
            pltpu.SemaphoreType.DMA((2, G)),
            pltpu.SemaphoreType.DMA((4,)),
        ],
        compiler_params=pltpu.CompilerParams(vmem_limit_bytes=LARGE),
        cost_estimate=pl.CostEstimate(
            flops=2 * 10**9, bytes_accessed=13 * 10**6, transcendentals=0
        ),
        name="pre",
    )(core, rates, hidden, w_bc, x, dy, codes)


def chip_kernel(mine_ref, got_ref, out_ref):
    for m in range(CHIPS):
        for i in range(GT):
            other = got_ref[m, STATE_ROWS + i : STATE_ROWS + i + 1, :]
            rows = slice(8 * i, 8 * i + 8)
            out_ref[m, rows, :] = other * mine_ref[m, rows, :] + got_ref[m, rows, :]
        tail = slice(STATE_ROWS, ROWS)
        out_ref[m, tail, :] = mine_ref[m, tail, :] * got_ref[m, tail, :]


def chip_sum(mine, got):
    return pl.pallas_call(
        chip_kernel,
        in_specs=[WHOLE, WHOLE],
        out_specs=WHOLE,
        out_shape=jax.ShapeDtypeStruct((CHIPS, ROWS, 128), F32),
        compiler_params=pltpu.CompilerParams(vmem_limit_bytes=SMALL),
        name="chip_sum",
    )(mine, got)


def scan_kernel(c_ref, in_ref, after_ref, out_ref):
    core = c_ref[0]
    state = [jnp.zeros((8, 128), F32) for _ in range(GT)]
    for k in range(CHIPS):
        at = k + core * (CHIPS - 1 - 2 * k)
        for i in range(GT):
            rows = slice(8 * i, 8 * i + 8)
            out_ref[at, rows, :] = state[i]
            decay = in_ref[at, STATE_ROWS + i : STATE_ROWS + i + 1, :]
            state[i] = decay * state[i] + in_ref[at, rows, :]


def scan_chips(core, slices, after):
    return pl.pallas_call(
        scan_kernel,
        in_specs=[IN_SMEM, WHOLE, IN_SMEM],
        out_specs=WHOLE,
        out_shape=jax.ShapeDtypeStruct((CHIPS, STATE_ROWS, 128), F32),
        compiler_params=pltpu.CompilerParams(vmem_limit_bytes=SMALL),
        name="scan_chips",
    )(core, slices, after)


SPANS = ((0, 256), (0, 128), (256, 128))
CHUNK = 128


def span_weights(cumt, onehot, start, size):
    lo = slice(start, start + size)
    hi = slice(start + size, start + 2 * size)
    edge = cumt[start + size - 1 : start + size, :]
    u_lo = spread(jnp.exp(edge - cumt[lo, :]), onehot)
    u_hi = spread(jnp.exp(cumt[hi, :] - edge), onehot)
    return lo, hi, u_lo, u_hi


def chunk_masks():
    t_at = lax.broadcasted_iota(jnp.int32, (CHUNK, CHUNK), 0)
    s_at = lax.broadcasted_iota(jnp.int32, (CHUNK, CHUNK), 1)
    return t_at >= s_at, s_at < PS


def chunk_decay(cumt, cum_ref, rows, h, lower):
    gap = cumt[rows, h : h + 1] - cum_ref[0, h : h + 1, rows]
    return jnp.exp(jnp.where(lower, gap, -jnp.inf))


def pairs_kernel(
    c_ref, bc_ref, x_ref, dy_ref, cum_ref, cumt_ref, hidden_ref, after_ref,
    wmine_ref, wother_ref, dbc_ref, turned_ref, token_ref, kmat,
):
    q = pl.program_id(0)
    is_first = c_ref[0] == 0

    @pl.when(q == 0)
    def _():
        kmat[...] = jnp.zeros_like(kmat)

    turned_ref[...] = hidden_ref[...].T
    onehot = spread_matrix()
    cumt = cumt_ref[0]
    x = x_ref[...].astype(F32)
    dy = dy_ref[...].astype(F32)
    wg = dy * spread(jnp.exp(cumt), onehot)
    wi = x * spread(jnp.exp(cumt[T - 1 : T, :] - cumt), onehot)
    wmine_ref[...] = jnp.where(is_first, wg, wi).astype(BF16)
    wother_ref[...] = jnp.where(is_first, wi, wg).astype(BF16)
    for start, size in SPANS:
        lo, hi, u_lo, u_hi = span_weights(cumt, onehot, start, size)
        kmat[hi, lo] += mm_nt((dy[hi, :] * u_hi).astype(BF16), (x[lo, :] * u_lo).astype(BF16))
    lower, first = chunk_masks()
    for chunk in range(T // CHUNK):
        rows = slice(chunk * CHUNK, (chunk + 1) * CHUNK)
        ksum = jnp.zeros((CHUNK, CHUNK), F32)
        for i in range(GT):
            lanes = slice(128 * i, 128 * i + 128)
            xt = x_ref[rows, lanes]
            dyf = dy[rows, lanes]
            for e in range(2):
                own = first if e == 0 else jnp.logical_not(first)
                dyh = jnp.where(own, dyf, 0.0).astype(BF16)
                ksum += chunk_decay(cumt, cum_ref, rows, 2 * i + e, lower) * mm_nt(dyh, xt)
        kmat[rows, rows] += ksum

    @pl.when(q == G - 1)
    def _():
        k = kmat[...].astype(BF16)
        dbc_ref[:, :N] = mm_tn(k, bc_ref[:, N:])
        dbc_ref[:, N:] = mm(k, bc_ref[:, :N])
        token_ref[0] = 0


def full_spec(*shape):
    return pl.BlockSpec(shape, lambda q: (0,) * len(shape))


def cols_spec(rows=T):
    return pl.BlockSpec((rows, GL), lambda q: (0, q))


def group_spec(*shape):
    return pl.BlockSpec((1, *shape), lambda q: (q, 0, 0))


def pairs(core, bc, x, dy, cum, cumt, hidden, after):
    return pl.pallas_call(
        pairs_kernel,
        grid=(G,),
        in_specs=[
            pl.BlockSpec(memory_space=pltpu.SMEM),
            full_spec(T, 2 * N),
            cols_spec(),
            cols_spec(),
            group_spec(16, T),
            group_spec(T, 128),
            cols_spec(),
            IN_HBM,
        ],
        out_specs=[
            cols_spec(),
            cols_spec(),
            full_spec(T, 2 * N),
            pl.BlockSpec((GL, T), lambda q: (q, 0)),
            IN_SMEM,
        ],
        out_shape=[
            jax.ShapeDtypeStruct((T, D), BF16),
            jax.ShapeDtypeStruct((T, D), BF16),
            jax.ShapeDtypeStruct((T, 2 * N), F32),
            jax.ShapeDtypeStruct((D, T), BF16),
            TOKEN,
        ],
        scratch_shapes=[pltpu.VMEM((T, T), F32)],
        compiler_params=pltpu.CompilerParams(vmem_limit_bytes=LARGE),
        cost_estimate=pl.CostEstimate(
            flops=20 * 10**9, bytes_accessed=16 * 10**6, transcendentals=3 * 10**6
        ),
        name="pairs",
    )(core, bc, x, dy, cum, cumt, hidden, after)


def carry_kernel(w_ref, came_ref, acc_ref, state_ref):
    acc = jnp.zeros((T, N), F32)
    for q in range(G):
        for i in range(GT):
            rows = slice(8 * i, 8 * i + 8)
            lanes = slice(GL * q + 128 * i, GL * q + 128 * i + 128)
            for m in range(0, NM, 2):
                at = NM * q + m
                pair = jnp.concatenate([came_ref[at, rows, :], came_ref[at + 1, rows, :]])
                state_ref[8 * m : 8 * m + 16, lanes] = pair.astype(BF16)
        cols = slice(GL * q, GL * (q + 1))
        acc += mm_nt(w_ref[:, cols], state_ref[:, cols])
    acc_ref[...] = acc


def carry(w_mine, came):
    return pl.pallas_call(
        carry_kernel,
        in_specs=[WHOLE, WHOLE],
        out_specs=[WHOLE, WHOLE],
        out_shape=[
            jax.ShapeDtypeStruct((T, N), F32),
            jax.ShapeDtypeStruct((N, D), BF16),
        ],
        compiler_params=pltpu.CompilerParams(vmem_limit_bytes=SMALL),
        cost_estimate=pl.CostEstimate(
            flops=4 * 10**8, bytes_accessed=5 * 10**6, transcendentals=0
        ),
        name="carry",
    )(w_mine, came)


def weight_kernel(
    c_ref, accmine_ref, wother_ref, came_ref, theirs_ref, dbc_ref, turned_hbm,
    gwmine_ref, gwother_ref, state_ref, turned_scr, sem,
):
    core = c_ref[0]
    is_first = core == 0
    starts = [pl.multiple_of(half * HALF_D, HALF_D) for half in (1 - core, core)]
    loads = [
        pltpu.make_async_copy(
            turned_hbm.at[pl.ds(start, HALF_D), :], turned_scr.at[n], sem.at[n]
        )
        for n, start in enumerate(starts)
    ]
    for load in loads:
        load.start()
    acc = jnp.zeros((T, N), F32)
    for q in range(G):
        for i in range(GT):
            rows = slice(8 * i, 8 * i + 8)
            lanes = slice(GL * q + 128 * i, GL * q + 128 * i + 128)
            tail = slice(STATE_ROWS + i, STATE_ROWS + i + 1)
            decay = theirs_ref[NM * q, tail, :]
            for m in range(0, NM, 2):
                at = NM * q + m
                pair = jnp.concatenate(
                    [
                        decay * came_ref[k, rows, :] + theirs_ref[k, rows, :]
                        for k in (at, at + 1)
                    ]
                )
                state_ref[8 * m : 8 * m + 16, lanes] = pair.astype(BF16)
        cols = slice(GL * q, GL * (q + 1))
        acc += mm_nt(wother_ref[:, cols], state_ref[:, cols])
    mine = accmine_ref[...]
    db = dbc_ref[:, :N] + jnp.where(is_first, acc, mine)
    dc = dbc_ref[:, N:] + jnp.where(is_first, mine, acc)
    dbc = (jnp.concatenate([db, dc], axis=1) * (1.0 / (T * 2 * CHIPS))).astype(BF16)
    for n, ref in enumerate((gwother_ref, gwmine_ref)):
        loads[n].wait()
        part = mm(turned_scr[n], dbc)
        ref[0] = part[:, :N]
        ref[1] = part[:, N:]


def weight_part(core, acc_mine, w_other, came, theirs, dbc, turned):
    return pl.pallas_call(
        weight_kernel,
        in_specs=[IN_SMEM] + [WHOLE] * 5 + [IN_HBM],
        out_specs=[WHOLE, WHOLE, WHOLE],
        out_shape=[
            jax.ShapeDtypeStruct((2, HALF_D, N), F32),
            jax.ShapeDtypeStruct((2, HALF_D, N), F32),
            jax.ShapeDtypeStruct((N, D), BF16),
        ],
        scratch_shapes=[
            pltpu.VMEM((2, HALF_D, T), BF16),
            pltpu.SemaphoreType.DMA((2,)),
        ],
        compiler_params=pltpu.CompilerParams(vmem_limit_bytes=MIDDLE),
        cost_estimate=pl.CostEstimate(
            flops=2 * 10**9, bytes_accessed=12 * 10**6, transcendentals=0
        ),
        name="weight_part",
    )(core, acc_mine, w_other, came, theirs, dbc, turned)


def outputs_kernel(
    c_ref, bc_ref, x_ref, dy_ref, cum_ref, cumt_ref, skip_ref, smine_ref, sother_ref, *refs,
):
    mixed_ref, gradx_ref, token_ref, scores, yacc, dxacc = refs[-6:]
    is_first = c_ref[0] == 0
    b_mat = bc_ref[:, :N]
    c_mat = bc_ref[:, N:]

    @pl.when(pl.program_id(0) == 0)
    def _():
        scores[...] = mm_nt(c_mat, b_mat)

    onehot = spread_matrix()
    cumt = cumt_ref[0]
    x = x_ref[...].astype(F32)
    dy = dy_ref[...].astype(F32)
    skip = skip_ref[...]
    mine = smine_ref[...].astype(F32)
    other = sother_ref[...].astype(F32)
    s_prev = jnp.where(is_first, mine, other).astype(BF16)
    g_next = jnp.where(is_first, other, mine).astype(BF16)
    fw = spread(jnp.exp(cumt), onehot)
    yacc[...] = skip * x + fw * mm(c_mat, s_prev)
    bw = spread(jnp.exp(cumt[T - 1 : T, :] - cumt), onehot)
    dxacc[...] = skip * dy + bw * mm(b_mat, g_next)
    for start, size in SPANS:
        lo, hi, u_lo, u_hi = span_weights(cumt, onehot, start, size)
        pair = scores[hi, lo].astype(BF16)
        yacc[hi, :] += u_hi * mm(pair, (x[lo, :] * u_lo).astype(BF16))
        dxacc[lo, :] += u_lo * mm_tn(pair, (dy[hi, :] * u_hi).astype(BF16))
    lower, first = chunk_masks()
    for chunk in range(T // CHUNK):
        rows = slice(chunk * CHUNK, (chunk + 1) * CHUNK)
        score = scores[rows, rows]
        for i in range(GT):
            lanes = slice(128 * i, 128 * i + 128)
            xt = x_ref[rows, lanes]
            dyt = dy_ref[rows, lanes]
            ys, dxs = [], []
            for e in range(2):
                decay = chunk_decay(cumt, cum_ref, rows, 2 * i + e, lower)
                mixing = (score * decay).astype(BF16)
                ys.append(mm(mixing, xt))
                dxs.append(mm_tn(mixing, dyt))
            mixed_ref[rows, lanes] = (
                yacc[rows, lanes] + jnp.where(first, ys[0], ys[1])
            ).astype(BF16)
            gradx_ref[rows, lanes] = (
                dxacc[rows, lanes] + jnp.where(first, dxs[0], dxs[1])
            ).astype(BF16)
    token_ref[0] = c_ref[0]


def outputs(core, bc, x, dy, cum, cumt, skip_row, s_mine, s_other, start, extra):
    cols = lambda rows=T: pl.BlockSpec((rows, GL), lambda q: (0, q + start))
    group = lambda *shape: pl.BlockSpec((1, *shape), lambda q: (q + start, 0, 0))
    return pl.pallas_call(
        outputs_kernel,
        grid=(G // 2,),
        in_specs=[
            IN_SMEM,
            full_spec(T, 2 * N),
            cols(),
            cols(),
            group(16, T),
            group(T, 128),
            cols(1),
            cols(N),
            cols(N),
        ]
        + [IN_HBM] * len(extra),
        out_specs=[cols(), cols(), IN_SMEM],
        out_shape=[
            jax.ShapeDtypeStruct((T, D), BF16),
            jax.ShapeDtypeStruct((T, D), BF16),
            TOKEN,
        ],
        scratch_shapes=[
            pltpu.VMEM((T, T), F32),
            pltpu.VMEM((T, GL), F32),
            pltpu.VMEM((T, GL), F32),
        ],
        input_output_aliases={9: 0, 10: 1} if len(extra) == 2 else {},
        compiler_params=pltpu.CompilerParams(vmem_limit_bytes=LARGE),
        cost_estimate=pl.CostEstimate(
            flops=12 * 10**9, bytes_accessed=7 * 10**6, transcendentals=2 * 10**6
        ),
        name="outputs",
    )(core, bc, x, dy, cum, cumt, skip_row, s_mine, s_other, *extra)


def add_kernel(a_ref, b_ref, out_hbm, scr, sem):
    block = HALF_D // 2
    stores = []
    for lane in range(2):
        for i in range(2):
            rows = pl.ds(block * i, block)
            scr[lane, rows, :] = a_ref[lane, rows, :] + b_ref[lane, rows, :]
            stores.append(
                pltpu.make_async_copy(
                    scr.at[lane, rows], out_hbm.at[lane, rows], sem.at[lane, i]
                )
            )
            stores[-1].start()
    for store in stores:
        store.wait()


def pair_add(a, b):
    return pl.pallas_call(
        add_kernel,
        in_specs=[WHOLE, WHOLE],
        out_specs=IN_HBM,
        out_shape=jax.ShapeDtypeStruct(a.shape, F32),
        scratch_shapes=[
            pltpu.VMEM(a.shape, F32),
            pltpu.SemaphoreType.DMA((2, 2)),
        ],
        compiler_params=pltpu.CompilerParams(vmem_limit_bytes=MIDDLE),
        name="pair_add",
    )(a, b)


def total_kernel(c_ref, in_ref, out_hbm, token_ref, scr, sem):
    total = jnp.sum(in_ref[...], axis=0)
    for k in range(NM // 2):
        scr[k] = total
    stores = [
        pltpu.make_async_copy(scr, out_hbm.at[pl.ds(NM // 2 * j, NM // 2)], sem.at[j])
        for j in range(2 * CHIPS // NM)
    ]
    for store in stores:
        store.start()
    token_ref[0] = c_ref[0]
    for store in stores:
        store.wait()


def chip_total(core, parts):
    return pl.pallas_call(
        total_kernel,
        in_specs=[IN_SMEM, WHOLE],
        out_specs=[IN_HBM, IN_SMEM],
        out_shape=[jax.ShapeDtypeStruct((CHIPS, GW_ROWS, 128), F32), TOKEN],
        scratch_shapes=[
            pltpu.VMEM((NM // 2, GW_ROWS, 128), F32),
            pltpu.SemaphoreType.DMA((2 * CHIPS // NM,)),
        ],
        compiler_params=pltpu.CompilerParams(vmem_limit_bytes=SMALL),
        name="chip_total",
    )(core, parts)


def hold_kernel(c_ref, in_ref, out_ref, token_ref):
    out_ref[...] = in_ref[...]
    token_ref[0] = c_ref[0]


def hold(core, half):
    return pl.pallas_call(
        hold_kernel,
        in_specs=[IN_SMEM, WHOLE],
        out_specs=[WHOLE, IN_SMEM],
        out_shape=[jax.ShapeDtypeStruct(half.shape, F32), TOKEN],
        compiler_params=pltpu.CompilerParams(vmem_limit_bytes=SMALL),
        name="hold",
    )(core, half)


def place_kernel(c_ref, half_ref, *refs):
    out_ref = refs[-1]
    for lane in range(2):
        out_ref[:, 128 * lane : 128 * lane + 128] = half_ref[lane]


def place(at, half, into):
    block = HALF_D // 2
    extra = [] if into is None else [into]
    return pl.pallas_call(
        place_kernel,
        grid_spec=pltpu.PrefetchScalarGridSpec(
            num_scalar_prefetch=1,
            grid=(2,),
            in_specs=[pl.BlockSpec((2, block, 128), lambda i, c: (0, i, 0))]
            + [pl.BlockSpec(memory_space=pl.ANY)] * len(extra),
            out_specs=pl.BlockSpec((block, 2 * N), lambda i, c: (2 * c[0] + i, 0)),
        ),
        out_shape=jax.ShapeDtypeStruct((D, 2 * N), F32),
        input_output_aliases={2: 0} if extra else {},
        compiler_params=pltpu.CompilerParams(vmem_limit_bytes=SMALL),
        name="place",
    )(at, half, *extra)


def swap(v):
    return lax.ppermute(v, "c", [(0, 1), (1, 0)])


def exchange(v):
    return lax.all_to_all(v, CHIP_AXES, 0, 0, tiled=True)


def shards(hidden, w_bc, ssm_in, codes, rates, skip, grad_out):
    core = lax.axis_index("c").astype(jnp.int32).reshape(1)
    skip_row = jnp.repeat(skip, PS)[None, :]
    bc, cum, cumt, mine, other = pre(
        core, hidden, w_bc, ssm_in, grad_out, codes, rates[None, :]
    )
    chip = chip_sum(mine, swap(other))
    slices = exchange(chip)
    theirs = swap(mine)
    w_mine, w_other, dbc, turned, paired = pairs(
        core, bc, ssm_in, grad_out, cum, cumt, hidden, chip
    )
    came = exchange(scan_chips(core, slices, paired))
    acc_mine, s_mine = carry(w_mine, came)
    gw_mine, gw_other, s_other = weight_part(
        core, acc_mine, w_other, swap(came), theirs, dbc, turned
    )
    part = pair_add(gw_mine, swap(gw_other))
    sums = exchange(part.reshape(CHIPS, GW_ROWS, 128))
    pieces = (bc, ssm_in, grad_out, cum, cumt, skip_row, s_mine, s_other)
    mixed, gradx, core_after = outputs(core, *pieces, 0, [part])
    total, core_after = chip_total(core_after, sums)
    half = exchange(total).reshape(2, HALF_D, 128)
    mixed, gradx, core_after = outputs(core_after, *pieces, G // 2, [mixed, gradx])
    half, core_after = hold(core_after, half)
    grad_w = place(1 - core, swap(half), place(core_after, half, None))
    return mixed, gradx, grad_w


def solution(mesh):
    grid = Mesh(mesh.devices.reshape(4, 4, 4, 2), ALL_AXES)
    rows = P(ALL_AXES, None)
    return jax.shard_map(
        shards,
        mesh=grid,
        in_specs=(rows, P(), rows, P(None, ALL_AXES), P(), P(), rows),
        out_specs=(rows, rows, P()),
        check_vma=False,
    )
```
